128 devices in a mesh: gz: 8 (over z, x_hi), gx: 16 (over x_lo, y, core).
Axes of the slice: x: 4 (x_hi: 2, x_lo: 2; x = x_hi * 2 + x_lo), y: 4, z: 4, core: 2. Of those that a mesh axis runs over, the one named last changes fastest.
Arguments:
- source: float32 [16, 4096, 4096], P(None, 'gx', 'gz'), may hold values from -6 to 6
Outputs:
- spectrum: float32 [16, 2, 2048, 4096], P('gx', None, None, 'gz')
The draws below stay inside these ranges and needn't reach their ends.
All inputs are finite; a program needn't handle non-finite values.
Results may differ from the reference program's by a relative error of at most 0.00007.
Values sent between devices are 32-bit elements; how exact they have to be, the bound alone decides.
A program may use at most 256 MiB of HBM per device.

```python
import math
import jax
import jax.numpy as jnp
from jax import lax

NY = 16
NZ = 4096
NX = 4096


def levels(key, dims, split, low, largest):
    factor_of, own = 1.0, jax.random.fold_in(key, 6)
    for dim, blocks in split:
        heights = jnp.exp(jax.random.uniform(jax.random.fold_in(own, dim), (blocks,), jnp.float32, low / len(split), largest / len(split)))
        factor_of = factor_of * jnp.repeat(heights, dims[dim] // blocks).reshape([-1 if axis == dim else 1 for axis in range(len(dims))])
    return factor_of


def bell_draw(stream_key, extent, width, most, split=(), kind=jnp.bfloat16):
    gain = levels(stream_key, extent, split, -0.22, 0.18) if split else 1.0
    values = jax.random.normal(stream_key, extent, jnp.float32) * width * gain
    return jnp.minimum(jnp.maximum(values, -most), most).astype(kind)


def setup_inputs(seed: int = 0) -> dict:
    streams_of = jax.random.split(jax.random.key(seed), 2)
    return {
        "source": bell_draw(streams_of[0], (NY, NX, NZ), 1.0, 6.0, ((1, 16), (2, 8)), jnp.float32),
    }


def one_plane(plane):
    length_x = plane.shape[0]
    length_z = plane.shape[1]
    folded = jnp.concatenate([plane[:, 0::2], plane[:, 1::2][:, ::-1]], axis=1)
    transformed = jnp.fft.fft(folded, axis=1)
    theta = math.pi / (2 * length_z) * jnp.arange(length_z, dtype=plane.dtype)
    cosine = 2.0 * (jnp.cos(theta) * transformed.real + jnp.sin(theta) * transformed.imag)
    periodic = jnp.fft.rfft(cosine, axis=0)
    half = length_x // 2
    real_part = periodic.real[:half]
    imag_part = periodic.imag[:half]
    imag_part = jnp.concatenate([periodic.real[half:half + 1], imag_part[1:]], axis=0)
    factor = 1.0 / math.sqrt(length_x * length_z)
    return jnp.stack([real_part, imag_part], axis=0) * factor

def reference(source):
    return lax.map(one_plane, source)
```

```python
import functools
import math

import jax
import jax.numpy as jnp
import ml_dtypes
import numpy as np
from jax import lax
from jax.experimental import pallas as pl
from jax.experimental.pallas import tpu as pltpu
from jax.sharding import PartitionSpec as P

MESH = pl.DeviceIdType.MESH
BF16 = jnp.bfloat16
F32 = jnp.float32
CHUNKS = 4
STEP = 53


def halves(table):
    high = table.astype(np.float32).astype(ml_dtypes.bfloat16)
    low = (table - high.astype(np.float64)).astype(np.float32).astype(ml_dtypes.bfloat16)
    return np.stack([high, low])


def span_tables(length, groups):
    wide = length // groups
    turns = 2 * groups
    each = length // turns // groups
    offset = np.arange(wide)
    table = np.zeros((groups, 2, wide, groups // 2, 2, 2, each))
    for p in range(groups):
        for tile in range(groups // 2):
            for half in range(2):
                block = 2 * tile + (half ^ (p % 2))
                for which in range(2):
                    residue = (p, turns - p)[which] if p else (0, groups)[which]
                    k = residue + turns * (block * each + np.arange(each))
                    angle = math.pi / (2 * length) * (np.outer(2 * offset + 1, k) % (4 * length))
                    if p:
                        table[p, 0, :, tile, half, which] = 2 * np.cos(angle)
                        table[p, 1, :, tile, half, which] = 2 * np.sin(angle) * (1 - 2 * which)
                    else:
                        table[p, which, :, tile, half, which] = 2 * np.cos(angle)
    return halves(table.reshape(groups, 2 * wide, wide))


def order_tables(length, groups):
    wide = length // groups
    turns = 2 * groups
    each = wide // turns
    out = np.zeros((2, wide, wide), np.float32)
    for odd in range(2):
        row = 0
        for u in range(groups // 2):
            for half in range(2):
                p = 2 * u + (half ^ odd)
                for which in range(2):
                    residue = (p, turns - p)[which] if p else (0, groups)[which]
                    for j in range(each):
                        out[odd, row, j * turns + residue] = 1.0
                        row += 1
    return out.astype(ml_dtypes.bfloat16)


def periodic_tables(length, groups, factor):
    wide = length // groups
    each = wide // 2
    r = np.arange(wide)
    table = np.zeros((groups // 2, 2, 2, each, 2, wide))
    for p in range(groups // 2):
        for which in range(2):
            residue = (p, groups - p)[which] if p else (0, groups // 2)[which]
            q = residue + groups * np.arange(each)
            angle = 2 * math.pi / length * (np.outer(q, r) % length)
            cos, sin = np.cos(angle) * factor, np.sin(angle) * factor
            if p:
                sign = 1 - 2 * which
                table[p, which, 0, :, 0] = cos
                table[p, which, 0, :, 1] = sin * sign
                table[p, which, 1, :, 0] = -sin
                table[p, which, 1, :, 1] = cos * sign
            else:
                table[p, which, 0, :, which] = cos
                table[p, which, 1, :, which] = -sin
    table[0, 0, 1, 0, 0] = (1 - 2 * (r % 2)) * factor
    return halves(table.reshape(groups // 2, 2 * wide, 2 * wide))


def split(value):
    high = value.astype(BF16)
    return high, (value - high.astype(F32)).astype(BF16)


def sixteenths(even, odd):
    root = math.sqrt(0.5)

    def parts(s):
        plus, minus = root * (s[1] + s[3]), root * (s[1] - s[3])
        return plus, minus

    out = [None] * 8
    s = even[0::2]
    t = even[1::2]
    p0, q0 = (s[0] + s[2]) + (s[1] + s[3]), (t[0] + t[2]) + (t[1] + t[3])
    p4, q4 = (s[0] + s[2]) - (s[1] + s[3]), (t[0] + t[2]) - (t[1] + t[3])
    out[0] = (p0 + q0, p0 - q0)
    out[4] = (p4, -q4)
    p2 = (s[0] - s[2], s[3] - s[1])
    q2 = (t[0] - t[2], t[3] - t[1])
    w2 = (root * (q2[0] + q2[1]), root * (q2[1] - q2[0]))
    out[2] = (p2[0] + w2[0], p2[1] + w2[1])
    out[6] = (p2[0] - w2[0], w2[1] - p2[1])
    s = odd[0::2]
    t = odd[1::2]
    s_plus, s_minus = parts(s)
    t_plus, t_minus = parts(t)
    p1, p3 = (s[0] + s_minus, -s[2] - s_plus), (s[0] - s_minus, s[2] - s_plus)
    q1, q3 = (t[0] + t_minus, -t[2] - t_plus), (t[0] - t_minus, t[2] - t_plus)
    for k, pk, qk in ((1, p1, q1), (3, p3, q3)):
        c, d = math.cos(math.pi * k / 8), math.sin(math.pi * k / 8)
        wk = (c * qk[0] + d * qk[1], c * qk[1] - d * qk[0])
        out[k] = (pk[0] + wk[0], pk[1] + wk[1])
        out[8 - k] = (pk[0] - wk[0], wk[1] - pk[1])
    return out


def dot(left, right):
    return jnp.dot(left, right, preferred_element_type=F32)


def span_kernel(
    source, table, order, pencil, got, tables, orders, high, low, result, cosine,
    barrier_free, table_sem, own_sem, send1, recv1, send2, recv2, own2,
):
    gz, gx = lax.axis_index("gz"), lax.axis_index("gx")
    z, x_ring, y, core = gz // 2, (gz % 2) * 2 + gx // 8, (gx // 2) % 4, gx % 2
    groups, planes = got.shape[1], got.shape[2]
    peers = groups * planes - 1

    barrier = pltpu.get_barrier_semaphore()

    def greet_span(t, carry):
        pl.semaphore_signal(barrier, inc=1, device_id=((gz + t) % groups, gx), device_id_type=MESH)
        return carry

    def greet_planes(t, carry):
        pl.semaphore_signal(barrier, inc=1, device_id=(gz, (gx + t) % planes), device_id_type=MESH)
        return carry

    lax.fori_loop(1, groups, greet_span, 0)
    lax.fori_loop(1, planes, greet_planes, 0)
    pl.semaphore_wait(barrier, groups + planes - 2)

    def rows_for(group, c):
        return source.at[:, pl.ds(pl.multiple_of(group * (CHUNKS * 8) + c * 8, 8), 8), :]

    def scatter(i, carry):
        c, t = i // (groups - 1), i % (groups - 1) + 1
        to = ((z + t // 2) % 4) * 2 + (gz + t) % 2
        pltpu.make_async_remote_copy(
            src_ref=rows_for(to, c),
            dst_ref=got.at[c, gz],
            send_sem=send1,
            recv_sem=recv1.at[c],
            device_id=(to, gx),
            device_id_type=MESH,
        ).start()
        return carry

    lax.fori_loop(0, CHUNKS * (groups - 1), scatter, 0)
    for c in range(CHUNKS):
        pltpu.make_async_copy(rows_for(gz, c), got.at[c, gz], own_sem.at[c]).start()
    table_copy = pltpu.make_async_copy(table, tables, table_sem.at[0])
    order_copy = pltpu.make_async_copy(order, orders, table_sem.at[1])
    table_copy.start()
    order_copy.start()
    table_copy.wait()
    order_copy.wait()

    lower = lax.broadcasted_iota(jnp.int32, (planes * 8, 128), 1) < 64

    def chunk(c, carry):
        pltpu.make_async_copy(got.at[c, 0 : groups - 1], got.at[c, 0 : groups - 1], recv1.at[c]).wait()
        pltpu.make_async_copy(rows_for(gz, c), got.at[c, gz], own_sem.at[c]).wait()

        def first(i, inner):
            rows = pl.ds(pl.multiple_of(i * 16, 16), 16)
            for lane in range(4):
                lanes = pl.ds(lane * 128, 128)
                s = [got[c, b, pl.ds(i * 2, 2), :, lanes].reshape(16, 128) for b in range(groups)]
                for p, pair in enumerate(sixteenths(s, s)):
                    for part in range(2):
                        at = pl.ds(part * 512 + lane * 128, 128)
                        high[p, rows, at], low[p, rows, at] = split(pair[part])
            return inner

        lax.fori_loop(0, planes // 2, first, 0)

        def second(p, inner):
            value = dot(high[p], tables[0, p]) + dot(low[p], tables[0, p])
            result[p] = value + dot(high[p], tables[1, p])
            return inner

        lax.fori_loop(0, groups, second, 0)

        def third(t, inner):
            lanes = pl.ds(pl.multiple_of(t * 128, 128), 128)
            found = [result[p, :, lanes] for p in range(groups)]
            for odd in range(2):
                mixed = jnp.concatenate(
                    [
                        jnp.where(lower, found[2 * u + odd], found[2 * u + 1 - odd])
                        for u in range(groups // 2)
                    ],
                    axis=1,
                )
                top, rest = split(mixed)
                cosine[c, 2 * t + odd] = dot(top, orders[odd]) + dot(rest, orders[odd])
            return inner

        lax.fori_loop(0, groups // 2, third, 0)

        def send(t, inner):
            o = (t * STEP) % peers + 1
            to_x = (x_ring + (o // 8) % 4) % 4
            to_gz = ((z + o // 32) % 4) * 2 + to_x // 2
            to_gx = (to_x % 2) * 8 + ((y + (o // 2) % 4) % 4) * 2 + (core + o) % 2
            pltpu.make_async_remote_copy(
                src_ref=cosine.at[c, to_gz, pl.ds(pl.multiple_of(to_gx * 8, 8), 8), :],
                dst_ref=pencil.at[gx * groups + gz, c],
                send_sem=send2.at[c],
                recv_sem=recv2.at[c],
                device_id=(to_gz, to_gx),
                device_id_type=MESH,
            ).start()
            return inner

        lax.fori_loop(0, peers, send, 0)
        pltpu.make_async_copy(
            cosine.at[c, gz, pl.ds(pl.multiple_of(gx * 8, 8), 8), :],
            pencil.at[gx * groups + gz, c],
            own2.at[c],
        ).start()
        return carry

    lax.fori_loop(0, CHUNKS, chunk, 0)

    everything = got.at[:, 0 : groups - 1]
    pltpu.make_async_copy(everything, everything, send1).wait()
    for c in range(CHUNKS):
        arrived = pencil.at[0:peers, c]
        pltpu.make_async_copy(arrived, arrived, recv2.at[c]).wait()
        pltpu.make_async_copy(arrived, arrived, send2.at[c]).wait()
        pltpu.make_async_copy(
            cosine.at[c, gz, pl.ds(pl.multiple_of(gx * 8, 8), 8), :],
            pencil.at[gx * groups + gz, c],
            own2.at[c],
        ).wait()


def periodic_kernel(lines, table, out, high, low, stage, sems):
    pairs, wide = high.shape[0], lines.shape[1]
    tiles = lines.shape[2] // 128
    step = pl.program_id(0)

    def first(i, carry):
        rows = pl.ds(pl.multiple_of(i * 16, 16), 16)
        for lane in range(tiles):
            lanes = pl.ds(lane * 128, 128)
            s = [lines[g, rows, lanes] for g in range(2 * pairs)]
            even = [s[g] + s[g + pairs] for g in range(pairs)]
            odd = [s[g] - s[g + pairs] for g in range(pairs)]
            for p, pair in enumerate(sixteenths(even, odd)):
                for part in range(2):
                    at = pl.ds(pl.multiple_of(part * wide + i * 16, 16), 16)
                    high[p, at, lanes], low[p, at, lanes] = split(pair[part])
        return carry

    lax.fori_loop(0, wide // 16, first, 0)
    each = wide // 2
    for p in range(pairs):
        value = dot(table[0, p], high[p]) + dot(table[0, p], low[p])
        value = value + dot(table[1, p], high[p])
        for which in range(2):
            residue = (p, 2 * pairs - p)[which] if p else (0, pairs)[which]
            for part in range(2):
                piece = value[(2 * which + part) * each : (2 * which + part + 1) * each]
                for lane in range(tiles):
                    at = pl.ds(residue, each, stride=2 * pairs)
                    stage[step, lane, part, at, :] = piece[:, lane * 128 : lane * 128 + 128]

    def leave(at, lane):
        lanes = pl.ds(pl.multiple_of((at * tiles + lane) * 128, 128), 128)
        return pltpu.make_async_copy(stage.at[at, lane], out.at[0, :, :, lanes], sems.at[at, lane])

    for lane in range(tiles):
        leave(step, lane).start()

    @pl.when(step == pl.num_programs(0) - 1)
    def _():
        for at in range(stage.shape[0]):
            for lane in range(tiles):
                leave(at, lane).wait()


def local(source):
    groups, across = lax.axis_size("gz"), lax.axis_size("gx")
    planes, rows, wide = source.shape
    span_total, periodic_total = wide * groups, rows * across
    table = jnp.asarray(span_tables(span_total, groups))
    order = jnp.asarray(order_tables(span_total, groups))
    any_spec = pl.BlockSpec(memory_space=pl.ANY)
    lines = planes * 8
    pencil = pl.pallas_call(
        span_kernel,
        out_shape=jax.ShapeDtypeStruct((across * groups, CHUNKS, 8, wide), F32),
        in_specs=[any_spec] * 3,
        out_specs=any_spec,
        scratch_shapes=[
            pltpu.VMEM((CHUNKS, groups, planes, 8, wide), F32),
            pltpu.VMEM(table.shape, BF16),
            pltpu.VMEM(order.shape, BF16),
            pltpu.VMEM((groups, lines, 2 * wide), BF16),
            pltpu.VMEM((groups, lines, 2 * wide), BF16),
            pltpu.VMEM((groups, lines, wide), F32),
            pltpu.VMEM((CHUNKS, groups, lines, wide), F32),
            pltpu.SemaphoreType.REGULAR,
            pltpu.SemaphoreType.DMA((2,)),
            pltpu.SemaphoreType.DMA((CHUNKS,)),
            pltpu.SemaphoreType.DMA,
            pltpu.SemaphoreType.DMA((CHUNKS,)),
            pltpu.SemaphoreType.DMA((CHUNKS,)),
            pltpu.SemaphoreType.DMA((CHUNKS,)),
            pltpu.SemaphoreType.DMA((CHUNKS,)),
        ],
        compiler_params=pltpu.CompilerParams(
            collective_id=0, has_side_effects=True, vmem_limit_bytes=60 * 2**20
        ),
        name="span",
    )(source, table, order)
    factor = 1.0 / math.sqrt(span_total * periodic_total)
    periodic = jnp.asarray(periodic_tables(periodic_total, across, factor))
    block = 256
    return pl.pallas_call(
        periodic_kernel,
        grid=(wide // block,),
        out_shape=jax.ShapeDtypeStruct((1, 2, periodic_total // 2, wide), F32),
        in_specs=[
            pl.BlockSpec((across, rows, block), lambda i: (0, 0, i)),
            pl.BlockSpec(periodic.shape, lambda i: (0, 0, 0, 0), pipeline_mode=pl.Buffered(1)),
        ],
        out_specs=any_spec,
        scratch_shapes=[
            pltpu.VMEM((across // 2, 2 * rows, block), BF16),
            pltpu.VMEM((across // 2, 2 * rows, block), BF16),
            pltpu.VMEM((wide // block, block // 128, 2, periodic_total // 2, 128), F32),
            pltpu.SemaphoreType.DMA((wide // block, block // 128)),
        ],
        compiler_params=pltpu.CompilerParams(vmem_limit_bytes=60 * 2**20),
        name="periodic",
    )(pencil.reshape(across, rows, wide), periodic)


def solution(mesh):
    return jax.shard_map(
        local,
        mesh=mesh,
        in_specs=(P(None, "gx", "gz"),),
        out_specs=P("gx", None, None, "gz"),
        check_vma=False,
    )
```

```python
import math

import jax
import jax.numpy as jnp
import ml_dtypes
import numpy as np
from jax import lax
from jax.experimental import pallas as pl
from jax.experimental.pallas import tpu as pltpu
from jax.sharding import PartitionSpec as P

MESH = pl.DeviceIdType.MESH
BF16 = jnp.bfloat16
F32 = jnp.float32
CHUNKS = 4
STEP = 41


def halves(table):
    high = table.astype(np.float32).astype(ml_dtypes.bfloat16)
    low = (table - high.astype(np.float64)).astype(np.float32).astype(ml_dtypes.bfloat16)
    return np.stack([high, low])


def span_tables(length, groups):
    wide = length // groups
    turns = 2 * groups
    each = length // turns // groups
    offset = np.arange(wide)
    table = np.zeros((groups, 2, wide, groups // 2, 2, 2, each))
    for p in range(groups):
        for tile in range(groups // 2):
            for half in range(2):
                block = 2 * tile + (half ^ (p % 2))
                for which in range(2):
                    residue = (p, turns - p)[which] if p else (0, groups)[which]
                    k = residue + turns * (block * each + np.arange(each))
                    angle = math.pi / (2 * length) * (np.outer(2 * offset + 1, k) % (4 * length))
                    if p:
                        table[p, 0, :, tile, half, which] = 2 * np.cos(angle)
                        table[p, 1, :, tile, half, which] = 2 * np.sin(angle) * (1 - 2 * which)
                    else:
                        table[p, which, :, tile, half, which] = 2 * np.cos(angle)
    return halves(table.reshape(groups, 2 * wide, wide))


def order_tables(length, groups):
    wide = length // groups
    turns = 2 * groups
    each = wide // turns
    out = np.zeros((2, wide, wide), np.float32)
    for odd in range(2):
        row = 0
        for u in range(groups // 2):
            for half in range(2):
                p = 2 * u + (half ^ odd)
                for which in range(2):
                    residue = (p, turns - p)[which] if p else (0, groups)[which]
                    for j in range(each):
                        out[odd, row, j * turns + residue] = 1.0
                        row += 1
    return out.astype(ml_dtypes.bfloat16)


def periodic_tables(length, groups, spans, factor):
    wide = length // groups
    each = wide // 2
    rest = wide // spans // CHUNKS
    r = np.arange(wide).reshape(spans, CHUNKS, rest).transpose(1, 0, 2).reshape(-1)
    table = np.zeros((groups // 2, 2, 2, each, 2, wide))
    for p in range(groups // 2):
        for which in range(2):
            residue = (p, groups - p)[which] if p else (0, groups // 2)[which]
            q = residue + groups * np.arange(each)
            angle = 2 * math.pi / length * (np.outer(q, r) % length)
            cos, sin = np.cos(angle) * factor, np.sin(angle) * factor
            if p:
                sign = 1 - 2 * which
                table[p, which, 0, :, 0] = cos
                table[p, which, 0, :, 1] = sin * sign
                table[p, which, 1, :, 0] = -sin
                table[p, which, 1, :, 1] = cos * sign
            else:
                table[p, which, 0, :, which] = cos
                table[p, which, 1, :, which] = -sin
    table[0, 0, 1, 0, 0] = (1 - 2 * (r % 2)) * factor
    high, low = halves(table.reshape(groups // 2, 2 * wide, 2 * wide))
    return np.concatenate([high, low], axis=1)


def split(value):
    high = value.astype(BF16)
    return high, (value - high.astype(F32)).astype(BF16)


def sixteenths(even, odd):
    root = math.sqrt(0.5)

    def parts(s):
        plus, minus = root * (s[1] + s[3]), root * (s[1] - s[3])
        return plus, minus

    out = [None] * 8
    s = even[0::2]
    t = even[1::2]
    p0, q0 = (s[0] + s[2]) + (s[1] + s[3]), (t[0] + t[2]) + (t[1] + t[3])
    p4, q4 = (s[0] + s[2]) - (s[1] + s[3]), (t[0] + t[2]) - (t[1] + t[3])
    out[0] = (p0 + q0, p0 - q0)
    out[4] = (p4, -q4)
    p2 = (s[0] - s[2], s[3] - s[1])
    q2 = (t[0] - t[2], t[3] - t[1])
    w2 = (root * (q2[0] + q2[1]), root * (q2[1] - q2[0]))
    out[2] = (p2[0] + w2[0], p2[1] + w2[1])
    out[6] = (p2[0] - w2[0], w2[1] - p2[1])
    s = odd[0::2]
    t = odd[1::2]
    s_plus, s_minus = parts(s)
    t_plus, t_minus = parts(t)
    p1, p3 = (s[0] + s_minus, -s[2] - s_plus), (s[0] - s_minus, s[2] - s_plus)
    q1, q3 = (t[0] + t_minus, -t[2] - t_plus), (t[0] - t_minus, t[2] - t_plus)
    for k, pk, qk in ((1, p1, q1), (3, p3, q3)):
        c, d = math.cos(math.pi * k / 8), math.sin(math.pi * k / 8)
        wk = (c * qk[0] + d * qk[1], c * qk[1] - d * qk[0])
        out[k] = (pk[0] + wk[0], pk[1] + wk[1])
        out[8 - k] = (pk[0] - wk[0], wk[1] - pk[1])
    return out


def dot(left, right):
    return jnp.dot(left, right, preferred_element_type=F32)


def kernel(
    source, span_table, order_table, periodic_table, out, got, tables, orders, high, low, result, cosine, pencil, stage,
    table_sem, own_sem, send1, recv1, send2, recv2, own2, out_sem,
):
    gz, gx = lax.axis_index("gz"), lax.axis_index("gx")
    z, x_ring, y, core = gz // 2, (gz % 2) * 2 + gx // 8, (gx // 2) % 4, gx % 2
    groups, planes, wide = got.shape[1], got.shape[2], got.shape[4]
    peers = groups * planes - 1
    last = CHUNKS - 1
    barrier = pltpu.get_barrier_semaphore()

    def greet_span(t, carry):
        pl.semaphore_signal(barrier, inc=1, device_id=((gz + t) % groups, gx), device_id_type=MESH)
        return carry

    def greet_planes(t, carry):
        pl.semaphore_signal(barrier, inc=1, device_id=(gz, (gx + t) % planes), device_id_type=MESH)
        return carry

    lax.fori_loop(1, groups, greet_span, 0)
    lax.fori_loop(1, planes, greet_planes, 0)
    pl.semaphore_wait(barrier, groups + planes - 2)

    def rows_for(group, c):
        return source.at[:, pl.ds(pl.multiple_of(group * (CHUNKS * 8) + c * 8, 8), 8), :]

    def scatter(i, carry):
        c, t = i // (groups - 1), i % (groups - 1) + 1
        to = ((z + t // 2) % 4) * 2 + (gz + t) % 2
        pltpu.make_async_remote_copy(
            src_ref=rows_for(to, c),
            dst_ref=got.at[c, gz],
            send_sem=send1,
            recv_sem=recv1.at[c],
            device_id=(to, gx),
            device_id_type=MESH,
        ).start()
        return carry

    lax.fori_loop(0, CHUNKS * (groups - 1), scatter, 0)
    for c in range(CHUNKS):
        pltpu.make_async_copy(rows_for(gz, c), got.at[c, gz], own_sem.at[c]).start()
    table_copy = pltpu.make_async_copy(span_table, tables, table_sem.at[0])
    order_copy = pltpu.make_async_copy(order_table, orders, table_sem.at[1])
    table_copy.start()
    order_copy.start()
    table_copy.wait()
    order_copy.wait()

    lower = lax.broadcasted_iota(jnp.int32, (planes * 8, 128), 1) < 64

    def take(c):
        pltpu.make_async_copy(got.at[c, 0 : groups - 1], got.at[c, 0 : groups - 1], recv1.at[c]).wait()
        pltpu.make_async_copy(rows_for(gz, c), got.at[c, gz], own_sem.at[c]).wait()

    def span_chunk(c):
        def first(i, inner):
            rows = pl.ds(pl.multiple_of(i * 16, 16), 16)
            for lane in range(wide // 128):
                lanes = pl.ds(lane * 128, 128)
                s = [got[c, b, pl.ds(i * 2, 2), :, lanes].reshape(16, 128) for b in range(groups)]
                for p, pair in enumerate(sixteenths(s, s)):
                    for part in range(2):
                        at = pl.ds(part * wide + lane * 128, 128)
                        high[p, rows, at], low[p, rows, at] = split(pair[part])
            return inner

        lax.fori_loop(0, planes // 2, first, 0)

        def second(p, inner):
            value = dot(high[p], tables[0, p]) + dot(low[p], tables[0, p])
            result[p] = value + dot(high[p], tables[1, p])
            return inner

        lax.fori_loop(0, groups, second, 0)

        def third(t, inner):
            lanes = pl.ds(pl.multiple_of(t * 128, 128), 128)
            found = [result[p, :, lanes] for p in range(groups)]
            for odd in range(2):
                mixed = jnp.concatenate(
                    [
                        jnp.where(lower, found[2 * u + odd], found[2 * u + 1 - odd])
                        for u in range(groups // 2)
                    ],
                    axis=1,
                )
                top, rest = split(mixed)
                cosine[c, 2 * t + odd] = dot(top, orders[odd]) + dot(rest, orders[odd])
            return inner

        lax.fori_loop(0, groups // 2, third, 0)

    def mine(c, lanes):
        return pltpu.make_async_copy(
            cosine.at[c, gz, pl.ds(pl.multiple_of(gx * 8, 8), 8), lanes],
            pencil.at[gx * groups + gz, c, :, lanes],
            own2.at[c],
        )

    def send(c, slot, lanes):
        def one(t, inner):
            o = (t * STEP) % peers + 1
            to_x = (x_ring + (o // 8) % 4) % 4
            to_gz = ((z + o // 32) % 4) * 2 + to_x // 2
            to_gx = (to_x % 2) * 8 + ((y + (o // 2) % 4) % 4) * 2 + (core + o) % 2
            pltpu.make_async_remote_copy(
                src_ref=cosine.at[c, to_gz, pl.ds(pl.multiple_of(to_gx * 8, 8), 8), lanes],
                dst_ref=pencil.at[gx * groups + gz, c, :, lanes],
                send_sem=send2.at[slot],
                recv_sem=recv2.at[slot],
                device_id=(to_gz, to_gx),
                device_id_type=MESH,
            ).start()
            return inner

        lax.fori_loop(0, peers, one, 0)

    every = pl.ds(0, wide)
    block = wide // 2
    sides = [pl.ds(h * block, block) for h in range(2)]

    def early(c, carry):
        take(c)
        span_chunk(c)
        mine(c, every).start()
        return carry

    lax.fori_loop(0, last, early, 0)
    send(0, 0, every)
    take(last)
    send(1, 1, every)
    span_chunk(last)
    mine(last, every).start()
    for c in range(2, last):
        send(c, c, every)
    for h in range(2):
        send(last, last + h, sides[h])

    periodic_copy = pltpu.make_async_copy(periodic_table, tables.at[0], table_sem.at[0])
    periodic_copy.start()
    pairs = planes // 2
    each = wide // 4

    def fold(c, tiles):
        def step(i, carry):
            for lane in tiles:
                lanes = pl.ds(lane * 128, 128)
                s = [pencil[pl.ds(g * groups + i * 2, 2), c, :, lanes].reshape(16, 128) for g in range(planes)]
                even = [s[g] + s[g + pairs] for g in range(pairs)]
                odd = [s[g] - s[g + pairs] for g in range(pairs)]
                for p, pair in enumerate(sixteenths(even, odd)):
                    for part in range(2):
                        at = part * (wide // 2) + c * (groups * 8) + i * 16
                        top = pl.ds(pl.multiple_of(at, 16), 16)
                        rest = pl.ds(pl.multiple_of(at + wide, 16), 16)
                        tables[1, p, top, lanes], tables[1, p, rest, lanes] = split(pair[part])
            return carry

        lax.fori_loop(0, groups // 2, step, 0)

    def arrived(c, slot, lanes):
        view = pencil.at[0:peers, c, :, lanes]
        return pltpu.make_async_copy(view, view, recv2.at[slot])

    def leave(lane):
        lanes = pl.ds(lane * 128, 128)
        return pltpu.make_async_copy(stage.at[lane], out.at[0, :, :, lanes], out_sem.at[lane])

    for c in range(last):
        arrived(c, c, every).wait()
        mine(c, every).wait()
        fold(c, range(wide // 128))
    mine(last, every).wait()
    periodic_copy.wait()
    for h in range(2):
        arrived(last, last + h, sides[h]).wait()
        tiles = range(h * block // 128, (h + 1) * block // 128)
        fold(last, tiles)
        for p in range(pairs):
            table_high, table_low = tables[0, p, 0:wide, :], tables[0, p, wide : 2 * wide, :]
            line_high, line_low = tables[1, p, 0:wide, sides[h]], tables[1, p, wide : 2 * wide, sides[h]]
            value = dot(table_high, line_high) + dot(table_high, line_low) + dot(table_low, line_high)
            for which in range(2):
                residue = (p, planes - p)[which] if p else (0, pairs)[which]
                for part in range(2):
                    piece = value[(2 * which + part) * each : (2 * which + part + 1) * each]
                    for n, lane in enumerate(tiles):
                        at = pl.ds(residue, each, stride=planes)
                        stage[lane, part, at, :] = piece[:, n * 128 : n * 128 + 128]
        for lane in tiles:
            leave(lane).start()

    everything = got.at[:, 0 : groups - 1]
    pltpu.make_async_copy(everything, everything, send1).wait()
    for slot in range(CHUNKS + 1):
        lanes = every if slot < last else sides[slot - last]
        view = pencil.at[0:peers, min(slot, last), :, lanes]
        pltpu.make_async_copy(view, view, send2.at[slot]).wait()
    for lane in range(wide // 128):
        leave(lane).wait()


def local(source):
    groups, across = lax.axis_size("gz"), lax.axis_size("gx")
    planes, rows, wide = source.shape
    span_total, periodic_total = wide * groups, rows * across
    factor = 1.0 / math.sqrt(span_total * periodic_total)
    table = jnp.asarray(span_tables(span_total, groups))
    order = jnp.asarray(order_tables(span_total, groups))
    periodic = jnp.asarray(periodic_tables(periodic_total, across, groups, factor))
    any_spec = pl.BlockSpec(memory_space=pl.ANY)
    lines = planes * 8
    half = periodic_total // 2
    return pl.pallas_call(
        kernel,
        out_shape=jax.ShapeDtypeStruct((1, 2, half, wide), F32),
        in_specs=[any_spec] * 4,
        out_specs=any_spec,
        scratch_shapes=[
            pltpu.VMEM((CHUNKS, groups, planes, 8, wide), F32),
            pltpu.VMEM(table.shape, BF16),
            pltpu.VMEM(order.shape, BF16),
            pltpu.VMEM((groups, lines, 2 * wide), BF16),
            pltpu.VMEM((groups, lines, 2 * wide), BF16),
            pltpu.VMEM((groups, lines, wide), F32),
            pltpu.VMEM((CHUNKS, groups, lines, wide), F32),
            pltpu.VMEM((across * groups, CHUNKS, 8, wide), F32),
            pltpu.VMEM((wide // 128, 2, half, 128), F32),
            pltpu.SemaphoreType.DMA((2,)),
            pltpu.SemaphoreType.DMA((CHUNKS,)),
            pltpu.SemaphoreType.DMA,
            pltpu.SemaphoreType.DMA((CHUNKS,)),
            pltpu.SemaphoreType.DMA((CHUNKS + 1,)),
            pltpu.SemaphoreType.DMA((CHUNKS + 1,)),
            pltpu.SemaphoreType.DMA((CHUNKS,)),
            pltpu.SemaphoreType.DMA((wide // 128,)),
        ],
        compiler_params=pltpu.CompilerParams(
            collective_id=0, has_side_effects=True, vmem_limit_bytes=62 * 2**20
        ),
        name="transform",
    )(source, table, order, periodic)


def solution(mesh):
    return jax.shard_map(
        local,
        mesh=mesh,
        in_specs=(P(None, "gx", "gz"),),
        out_specs=P("gx", None, None, "gz"),
        check_vma=False,
    )
```

```python
import math

import jax
import jax.numpy as jnp
import ml_dtypes
import numpy as np
from jax import lax
from jax.experimental import pallas as pl
from jax.experimental.pallas import tpu as pltpu
from jax.sharding import PartitionSpec as P

MESH = pl.DeviceIdType.MESH
BF16 = jnp.bfloat16
F32 = jnp.float32
CHUNKS = 4
STEP = 41


def halves(table):
    high = table.astype(np.float32).astype(ml_dtypes.bfloat16)
    low = (table - high.astype(np.float64)).astype(np.float32).astype(ml_dtypes.bfloat16)
    return np.stack([high, low])


def span_tables(length, groups):
    wide = length // groups
    turns = 2 * groups
    each = length // turns // groups
    offset = np.arange(wide)
    table = np.zeros((groups, 2, wide, groups // 2, 2, 2, each))
    for p in range(groups):
        for tile in range(groups // 2):
            for half in range(2):
                block = 2 * tile + (half ^ (p % 2))
                for which in range(2):
                    residue = (p, turns - p)[which] if p else (0, groups)[which]
                    k = residue + turns * (block * each + np.arange(each))
                    angle = math.pi / (2 * length) * (np.outer(2 * offset + 1, k) % (4 * length))
                    if p:
                        table[p, 0, :, tile, half, which] = 2 * np.cos(angle)
                        table[p, 1, :, tile, half, which] = 2 * np.sin(angle) * (1 - 2 * which)
                    else:
                        table[p, which, :, tile, half, which] = 2 * np.cos(angle)
    return halves(table.reshape(groups, 2 * wide, wide))


def order_tables(length, groups):
    wide = length // groups
    turns = 2 * groups
    each = wide // turns
    out = np.zeros((2, wide, wide), np.float32)
    for odd in range(2):
        row = 0
        for u in range(groups // 2):
            for half in range(2):
                p = 2 * u + (half ^ odd)
                for which in range(2):
                    residue = (p, turns - p)[which] if p else (0, groups)[which]
                    for j in range(each):
                        out[odd, row, j * turns + residue] = 1.0
                        row += 1
    return out.astype(ml_dtypes.bfloat16)


def periodic_tables(length, groups, spans, factor):
    wide = length // groups
    each = wide // 2
    rest = wide // spans // CHUNKS
    r = np.arange(wide).reshape(spans, CHUNKS, rest).transpose(1, 0, 2).reshape(-1)
    table = np.zeros((groups // 2, 2, 2, each, 2, wide))
    for p in range(groups // 2):
        for which in range(2):
            residue = (p, groups - p)[which] if p else (0, groups // 2)[which]
            q = residue + groups * np.arange(each)
            angle = 2 * math.pi / length * (np.outer(q, r) % length)
            cos, sin = np.cos(angle) * factor, np.sin(angle) * factor
            if p:
                sign = 1 - 2 * which
                table[p, which, 0, :, 0] = cos
                table[p, which, 0, :, 1] = sin * sign
                table[p, which, 1, :, 0] = -sin
                table[p, which, 1, :, 1] = cos * sign
            else:
                table[p, which, 0, :, which] = cos
                table[p, which, 1, :, which] = -sin
    table[0, 0, 1, 0, 0] = (1 - 2 * (r % 2)) * factor
    cut = wide - wide // CHUNKS
    table = table.reshape(groups // 2, 2 * wide, 2, wide)
    table = [t.reshape(groups // 2, 2 * wide, -1) for t in (table[..., :cut], table[..., cut:])]
    high, low = halves(np.concatenate(table, axis=-1))
    return np.concatenate([high, low], axis=1)


def split(value):
    high = value.astype(BF16)
    return high, (value - high.astype(F32)).astype(BF16)


def sixteenths(even, odd):
    root = math.sqrt(0.5)

    def parts(s):
        plus, minus = root * (s[1] + s[3]), root * (s[1] - s[3])
        return plus, minus

    out = [None] * 8
    s = even[0::2]
    t = even[1::2]
    p0, q0 = (s[0] + s[2]) + (s[1] + s[3]), (t[0] + t[2]) + (t[1] + t[3])
    p4, q4 = (s[0] + s[2]) - (s[1] + s[3]), (t[0] + t[2]) - (t[1] + t[3])
    out[0] = (p0 + q0, p0 - q0)
    out[4] = (p4, -q4)
    p2 = (s[0] - s[2], s[3] - s[1])
    q2 = (t[0] - t[2], t[3] - t[1])
    w2 = (root * (q2[0] + q2[1]), root * (q2[1] - q2[0]))
    out[2] = (p2[0] + w2[0], p2[1] + w2[1])
    out[6] = (p2[0] - w2[0], w2[1] - p2[1])
    s = odd[0::2]
    t = odd[1::2]
    s_plus, s_minus = parts(s)
    t_plus, t_minus = parts(t)
    p1, p3 = (s[0] + s_minus, -s[2] - s_plus), (s[0] - s_minus, s[2] - s_plus)
    q1, q3 = (t[0] + t_minus, -t[2] - t_plus), (t[0] - t_minus, t[2] - t_plus)
    for k, pk, qk in ((1, p1, q1), (3, p3, q3)):
        c, d = math.cos(math.pi * k / 8), math.sin(math.pi * k / 8)
        wk = (c * qk[0] + d * qk[1], c * qk[1] - d * qk[0])
        out[k] = (pk[0] + wk[0], pk[1] + wk[1])
        out[8 - k] = (pk[0] - wk[0], wk[1] - pk[1])
    return out


def dot(left, right):
    return jnp.dot(left, right, preferred_element_type=F32)


def kernel(
    source, span_table, order_table, periodic_table, stage, got, tables, orders, high, low, result, cosine, pencil,
    table_sem, own_sem, send1, recv1, send2, recv2, own2,
):
    gz, gx = lax.axis_index("gz"), lax.axis_index("gx")
    z, x_ring, y, core = gz // 2, (gz % 2) * 2 + gx // 8, (gx // 2) % 4, gx % 2
    groups, planes, wide = got.shape[1], got.shape[2], got.shape[4]
    peers = groups * planes - 1
    last = CHUNKS - 1
    barrier = pltpu.get_barrier_semaphore()

    def greet_span(t, carry):
        pl.semaphore_signal(barrier, inc=1, device_id=((gz + t) % groups, gx), device_id_type=MESH)
        return carry

    def greet_planes(t, carry):
        pl.semaphore_signal(barrier, inc=1, device_id=(gz, (gx + t) % planes), device_id_type=MESH)
        return carry

    lax.fori_loop(1, groups, greet_span, 0)
    lax.fori_loop(1, planes, greet_planes, 0)
    pl.semaphore_wait(barrier, groups + planes - 2)

    def rows_for(group, c):
        return source.at[:, pl.ds(pl.multiple_of(group * (CHUNKS * 8) + c * 8, 8), 8), :]

    def scatter(i, carry):
        c, t = i // (groups - 1), i % (groups - 1) + 1
        to = ((z + t // 2) % 4) * 2 + (gz + t) % 2
        pltpu.make_async_remote_copy(
            src_ref=rows_for(to, c),
            dst_ref=got.at[c, gz],
            send_sem=send1,
            recv_sem=recv1.at[c],
            device_id=(to, gx),
            device_id_type=MESH,
        ).start()
        return carry

    lax.fori_loop(0, CHUNKS * (groups - 1), scatter, 0)
    for c in range(CHUNKS):
        pltpu.make_async_copy(rows_for(gz, c), got.at[c, gz], own_sem.at[c]).start()
    table_copy = pltpu.make_async_copy(span_table, tables, table_sem.at[0])
    order_copy = pltpu.make_async_copy(order_table, orders, table_sem.at[1])
    table_copy.start()
    order_copy.start()
    table_copy.wait()
    order_copy.wait()

    lower = lax.broadcasted_iota(jnp.int32, (planes * 8, 128), 1) < 64

    def take(c):
        pltpu.make_async_copy(got.at[c, 0 : groups - 1], got.at[c, 0 : groups - 1], recv1.at[c]).wait()
        pltpu.make_async_copy(rows_for(gz, c), got.at[c, gz], own_sem.at[c]).wait()

    def span_chunk(c):
        def first(i, inner):
            rows = pl.ds(pl.multiple_of(i * 16, 16), 16)
            for lane in range(wide // 128):
                lanes = pl.ds(lane * 128, 128)
                s = [got[c, b, pl.ds(i * 2, 2), :, lanes].reshape(16, 128) for b in range(groups)]
                for p, pair in enumerate(sixteenths(s, s)):
                    for part in range(2):
                        at = pl.ds(part * wide + lane * 128, 128)
                        high[p, rows, at], low[p, rows, at] = split(pair[part])
            return inner

        lax.fori_loop(0, planes // 2, first, 0)

        def second(p, inner):
            value = dot(high[p], tables[0, p]) + dot(low[p], tables[0, p])
            result[p] = value + dot(high[p], tables[1, p])
            return inner

        lax.fori_loop(0, groups, second, 0)

        def third(t, inner):
            lanes = pl.ds(pl.multiple_of(t * 128, 128), 128)
            found = [result[p, :, lanes] for p in range(groups)]
            for odd in range(2):
                mixed = jnp.concatenate(
                    [
                        jnp.where(lower, found[2 * u + odd], found[2 * u + 1 - odd])
                        for u in range(groups // 2)
                    ],
                    axis=1,
                )
                top, rest = split(mixed)
                cosine[c, 2 * t + odd] = dot(top, orders[odd]) + dot(rest, orders[odd])
            return inner

        lax.fori_loop(0, groups // 2, third, 0)

    def mine(c, lanes):
        return pltpu.make_async_copy(
            cosine.at[c, gz, pl.ds(pl.multiple_of(gx * 8, 8), 8), lanes],
            pencil.at[gx * groups + gz, c, :, lanes],
            own2.at[c],
        )

    def send(c, slot, lanes):
        def one(t, inner):
            o = (t * STEP) % peers + 1
            to_x = (x_ring + (o // 8) % 4) % 4
            to_gz = ((z + o // 32) % 4) * 2 + to_x // 2
            to_gx = (to_x % 2) * 8 + ((y + (o // 2) % 4) % 4) * 2 + (core + o) % 2
            pltpu.make_async_remote_copy(
                src_ref=cosine.at[c, to_gz, pl.ds(pl.multiple_of(to_gx * 8, 8), 8), lanes],
                dst_ref=pencil.at[gx * groups + gz, c, :, lanes],
                send_sem=send2.at[slot],
                recv_sem=recv2.at[slot],
                device_id=(to_gz, to_gx),
                device_id_type=MESH,
            ).start()
            return inner

        lax.fori_loop(0, peers, one, 0)

    every = pl.ds(0, wide)
    block = wide // 2
    sides = [pl.ds(h * block, block) for h in range(2)]

    def early(c, carry):
        take(c)
        span_chunk(c)
        mine(c, every).start()
        return carry

    lax.fori_loop(0, last, early, 0)
    send(0, 0, every)
    take(last)
    send(1, 1, every)
    span_chunk(last)
    mine(last, every).start()
    for c in range(2, last):
        send(c, c, every)
    for h in range(2):
        send(last, last + h, sides[h])

    periodic_copy = pltpu.make_async_copy(periodic_table, tables.at[0], table_sem.at[0])
    periodic_copy.start()
    pairs = planes // 2
    each = wide // 4
    main = 2 * last * groups * 8

    def fold(c, tiles):
        def step(i, carry):
            for lane in tiles:
                lanes = pl.ds(lane * 128, 128)
                s = [pencil[pl.ds(g * groups + i * 2, 2), c, :, lanes].reshape(16, 128) for g in range(planes)]
                even = [s[g] + s[g + pairs] for g in range(pairs)]
                odd = [s[g] - s[g + pairs] for g in range(pairs)]
                for p, pair in enumerate(sixteenths(even, odd)):
                    for part in range(2):
                        at = part * (groups * 8) + (main if c == last else part * (main // 2 - groups * 8) + c * (groups * 8)) + i * 16
                        top = pl.ds(pl.multiple_of(at, 16), 16)
                        rest = pl.ds(pl.multiple_of(at + wide, 16), 16)
                        tables[1, p, top, lanes], tables[1, p, rest, lanes] = split(pair[part])
            return carry

        lax.fori_loop(0, groups // 2, step, 0)

    def arrived(c, slot, lanes):
        view = pencil.at[0:peers, c, :, lanes]
        return pltpu.make_async_copy(view, view, recv2.at[slot])

    for c in range(last):
        arrived(c, c, every).wait()
        mine(c, every).wait()
        fold(c, range(wide // 128))
    periodic_copy.wait()

    def gather(p, carry):
        table_high, table_low = tables[0, p, 0:wide, 0:main], tables[0, p, wide : 2 * wide, 0:main]
        for side in sides:
            line_high, line_low = tables[1, p, 0:main, side], tables[1, p, wide : wide + main, side]
            value = dot(table_high, line_high) + dot(table_high, line_low) + dot(table_low, line_high)
            for k in range(4):
                piece = value[k * each : (k + 1) * each].reshape(planes, 8, block)
                got[p // 2, (p % 2) * 4 + k, :, :, side] = piece
        return carry

    lax.fori_loop(0, pairs, gather, 0)
    mine(last, every).wait()
    for h in range(2):
        arrived(last, last + h, sides[h]).wait()
        tiles = range(h * block // 128, (h + 1) * block // 128)
        fold(last, tiles)
        for p in range(pairs):
            table_high, table_low = tables[0, p, 0:wide, main:wide], tables[0, p, wide : 2 * wide, main:wide]
            line_high, line_low = tables[1, p, main:wide, sides[h]], tables[1, p, wide + main : 2 * wide, sides[h]]
            value = dot(
                jnp.concatenate([table_high, table_high], axis=1),
                jnp.concatenate([line_high, line_low], axis=0),
            ) + dot(table_low, line_high)
            for which in range(2):
                residue = (p, planes - p)[which] if p else (0, pairs)[which]
                for part in range(2):
                    k = 2 * which + part
                    before = got[p // 2, (p % 2) * 4 + k, :, :, sides[h]].reshape(each, block)
                    piece = value[k * each : (k + 1) * each] + before
                    for n, lane in enumerate(tiles):
                        at = pl.ds(residue, each, stride=planes)
                        stage[lane, part, at, :] = piece[:, n * 128 : n * 128 + 128]

    everything = got.at[:, 0 : groups - 1]
    pltpu.make_async_copy(everything, everything, send1).wait()
    for slot in range(CHUNKS + 1):
        lanes = every if slot < last else sides[slot - last]
        view = pencil.at[0:peers, min(slot, last), :, lanes]
        pltpu.make_async_copy(view, view, send2.at[slot]).wait()


def place(tiles, out, sems):
    copies = [
        pltpu.make_async_copy(
            tiles.at[lane, part], out.at[0, part, :, pl.ds(lane * 128, 128)], sems.at[lane, part]
        )
        for lane in range(tiles.shape[0])
        for part in range(2)
    ]
    for copy in copies:
        copy.start()
    for copy in copies:
        copy.wait()


def local(source):
    groups, across = lax.axis_size("gz"), lax.axis_size("gx")
    planes, rows, wide = source.shape
    span_total, periodic_total = wide * groups, rows * across
    factor = 1.0 / math.sqrt(span_total * periodic_total)
    table = jnp.asarray(span_tables(span_total, groups))
    order = jnp.asarray(order_tables(span_total, groups))
    periodic = jnp.asarray(periodic_tables(periodic_total, across, groups, factor))
    any_spec = pl.BlockSpec(memory_space=pl.ANY)
    lines = planes * 8
    half = periodic_total // 2
    tiles = pl.pallas_call(
        kernel,
        out_shape=pltpu.VMEM((wide // 128, 2, half, 128), F32),
        in_specs=[any_spec] * 4,
        out_specs=pl.BlockSpec(memory_space=pltpu.VMEM),
        scratch_shapes=[
            pltpu.VMEM((CHUNKS, groups, planes, 8, wide), F32),
            pltpu.VMEM(table.shape, BF16),
            pltpu.VMEM(order.shape, BF16),
            pltpu.VMEM((groups, lines, 2 * wide), BF16),
            pltpu.VMEM((groups, lines, 2 * wide), BF16),
            pltpu.VMEM((groups, lines, wide), F32),
            pltpu.VMEM((CHUNKS, groups, lines, wide), F32),
            pltpu.VMEM((across * groups, CHUNKS, 8, wide), F32),
            pltpu.SemaphoreType.DMA((2,)),
            pltpu.SemaphoreType.DMA((CHUNKS,)),
            pltpu.SemaphoreType.DMA,
            pltpu.SemaphoreType.DMA((CHUNKS,)),
            pltpu.SemaphoreType.DMA((CHUNKS + 1,)),
            pltpu.SemaphoreType.DMA((CHUNKS + 1,)),
            pltpu.SemaphoreType.DMA((CHUNKS,)),
        ],
        compiler_params=pltpu.CompilerParams(
            collective_id=0, has_side_effects=True, vmem_limit_bytes=48 * 2**20
        ),
        name="transform",
    )(source, table, order, periodic)
    return pl.pallas_call(
        place,
        out_shape=jax.ShapeDtypeStruct((1, 2, half, wide), F32),
        in_specs=[any_spec],
        out_specs=any_spec,
        scratch_shapes=[pltpu.SemaphoreType.DMA((wide // 128, 2))],
        compiler_params=pltpu.CompilerParams(vmem_limit_bytes=4 * 2**20),
        name="place",
    )(pltpu.with_memory_space_constraint(tiles, pltpu.VMEM))


def solution(mesh):
    return jax.shard_map(
        local,
        mesh=mesh,
        in_specs=(P(None, "gx", "gz"),),
        out_specs=P("gx", None, None, "gz"),
        check_vma=False,
    )
```

```python
import math

import jax
import jax.numpy as jnp
import ml_dtypes
import numpy as np
from jax import lax
from jax.experimental import pallas as pl
from jax.experimental.pallas import tpu as pltpu
from jax.sharding import PartitionSpec as P

MESH = pl.DeviceIdType.MESH
BF16 = jnp.bfloat16
F32 = jnp.float32
CHUNKS = 4
PIECES = 16
STEP = 41


def halves(table):
    high = table.astype(np.float32).astype(ml_dtypes.bfloat16)
    low = (table - high.astype(np.float64)).astype(np.float32).astype(ml_dtypes.bfloat16)
    return np.stack([high, low])


def span_tables(length, groups):
    wide = length // groups
    turns = 2 * groups
    each = length // turns // groups
    offset = np.arange(wide)
    table = np.zeros((groups, 2, wide, groups // 2, 2, 2, each))
    for p in range(groups):
        for tile in range(groups // 2):
            for half in range(2):
                block = 2 * tile + (half ^ (p % 2))
                for which in range(2):
                    residue = (p, turns - p)[which] if p else (0, groups)[which]
                    k = residue + turns * (block * each + np.arange(each))
                    angle = math.pi / (2 * length) * (np.outer(2 * offset + 1, k) % (4 * length))
                    if p:
                        table[p, 0, :, tile, half, which] = 2 * np.cos(angle)
                        table[p, 1, :, tile, half, which] = 2 * np.sin(angle) * (1 - 2 * which)
                    else:
                        table[p, which, :, tile, half, which] = 2 * np.cos(angle)
    return halves(table.reshape(groups, 2 * wide, wide))


def order_tables(length, groups):
    wide = length // groups
    turns = 2 * groups
    each = wide // turns
    out = np.zeros((2, wide, wide), np.float32)
    for odd in range(2):
        row = 0
        for u in range(groups // 2):
            for half in range(2):
                p = 2 * u + (half ^ odd)
                for which in range(2):
                    residue = (p, turns - p)[which] if p else (0, groups)[which]
                    for j in range(each):
                        out[odd, row, j * turns + residue] = 1.0
                        row += 1
    return out.astype(ml_dtypes.bfloat16)


def periodic_tables(length, groups, spans, factor):
    wide = length // groups
    each = wide // 2
    rest = wide // spans // CHUNKS
    r = np.arange(wide).reshape(spans, CHUNKS, rest).transpose(1, 0, 2).reshape(-1)
    table = np.zeros((groups // 2, 2, 2, each, 2, wide))
    for p in range(groups // 2):
        for which in range(2):
            residue = (p, groups - p)[which] if p else (0, groups // 2)[which]
            q = residue + groups * np.arange(each)
            angle = 2 * math.pi / length * (np.outer(q, r) % length)
            cos, sin = np.cos(angle) * factor, np.sin(angle) * factor
            if p:
                sign = 1 - 2 * which
                table[p, which, 0, :, 0] = cos
                table[p, which, 0, :, 1] = sin * sign
                table[p, which, 1, :, 0] = -sin
                table[p, which, 1, :, 1] = cos * sign
            else:
                table[p, which, 0, :, which] = cos
                table[p, which, 1, :, which] = -sin
    table[0, 0, 1, 0, 0] = (1 - 2 * (r % 2)) * factor
    cut = wide - wide // CHUNKS
    table = table.reshape(groups // 2, 2 * wide, 2, wide)
    table = [t.reshape(groups // 2, 2 * wide, -1) for t in (table[..., :cut], table[..., cut:])]
    high, low = halves(np.concatenate(table, axis=-1))
    return np.concatenate([high, low], axis=1)


def split(value):
    high = value.astype(BF16)
    return high, (value - high.astype(F32)).astype(BF16)


def sixteenths(even, odd):
    root = math.sqrt(0.5)

    def parts(s):
        plus, minus = root * (s[1] + s[3]), root * (s[1] - s[3])
        return plus, minus

    out = [None] * 8
    s = even[0::2]
    t = even[1::2]
    p0, q0 = (s[0] + s[2]) + (s[1] + s[3]), (t[0] + t[2]) + (t[1] + t[3])
    p4, q4 = (s[0] + s[2]) - (s[1] + s[3]), (t[0] + t[2]) - (t[1] + t[3])
    out[0] = (p0 + q0, p0 - q0)
    out[4] = (p4, -q4)
    p2 = (s[0] - s[2], s[3] - s[1])
    q2 = (t[0] - t[2], t[3] - t[1])
    w2 = (root * (q2[0] + q2[1]), root * (q2[1] - q2[0]))
    out[2] = (p2[0] + w2[0], p2[1] + w2[1])
    out[6] = (p2[0] - w2[0], w2[1] - p2[1])
    s = odd[0::2]
    t = odd[1::2]
    s_plus, s_minus = parts(s)
    t_plus, t_minus = parts(t)
    p1, p3 = (s[0] + s_minus, -s[2] - s_plus), (s[0] - s_minus, s[2] - s_plus)
    q1, q3 = (t[0] + t_minus, -t[2] - t_plus), (t[0] - t_minus, t[2] - t_plus)
    for k, pk, qk in ((1, p1, q1), (3, p3, q3)):
        c, d = math.cos(math.pi * k / 8), math.sin(math.pi * k / 8)
        wk = (c * qk[0] + d * qk[1], c * qk[1] - d * qk[0])
        out[k] = (pk[0] + wk[0], pk[1] + wk[1])
        out[8 - k] = (pk[0] - wk[0], wk[1] - pk[1])
    return out


def dot(left, right):
    return jnp.dot(left, right, preferred_element_type=F32)


def kernel(
    source, span_table, order_table, periodic_table, stage, got, tables, orders, high, low, result, cosine, pencil,
    table_sem, own_sem, send1, recv1, send2, recv2, own2,
):
    gz, gx = lax.axis_index("gz"), lax.axis_index("gx")
    z, x_ring, y, core = gz // 2, (gz % 2) * 2 + gx // 8, (gx // 2) % 4, gx % 2
    groups, planes, wide = got.shape[1], got.shape[2], got.shape[4]
    peers = groups * planes - 1
    last = CHUNKS - 1

    def rows_for(group, c, start, size):
        return source.at[pl.ds(start, size), pl.ds(pl.multiple_of(group * (CHUNKS * 8) + c * 8, 8), 8), :]

    for c in range(CHUNKS):
        pltpu.make_async_copy(rows_for(gz, c, 0, planes), got.at[c, gz], own_sem.at[c]).start()
    table_copy = pltpu.make_async_copy(span_table, tables, table_sem.at[0])
    order_copy = pltpu.make_async_copy(order_table, orders, table_sem.at[1])
    table_copy.start()
    order_copy.start()
    barrier = pltpu.get_barrier_semaphore()

    def greet_span(t, carry):
        pl.semaphore_signal(barrier, inc=1, device_id=((gz + t) % groups, gx), device_id_type=MESH)
        return carry

    def greet_planes(t, carry):
        pl.semaphore_signal(barrier, inc=1, device_id=(gz, (gx + t) % planes), device_id_type=MESH)
        return carry

    lax.fori_loop(1, groups, greet_span, 0)
    lax.fori_loop(1, planes, greet_planes, 0)
    pl.semaphore_wait(barrier, groups + planes - 2)

    size = planes // PIECES

    def scatter(i, carry):
        c, start, t = i // (groups - 1) // PIECES, (i // (groups - 1)) % PIECES * size, i % (groups - 1) + 1
        to = ((z + t // 2) % 4) * 2 + (gz + t) % 2
        pltpu.make_async_remote_copy(
            src_ref=rows_for(to, c, start, size),
            dst_ref=got.at[c, gz, pl.ds(start, size)],
            send_sem=send1,
            recv_sem=recv1.at[c],
            device_id=(to, gx),
            device_id_type=MESH,
        ).start()
        return carry

    lax.fori_loop(0, CHUNKS * PIECES * (groups - 1), scatter, 0)
    table_copy.wait()
    order_copy.wait()

    lower = lax.broadcasted_iota(jnp.int32, (planes * 8, 128), 1) < 64

    def take(c):
        pltpu.make_async_copy(got.at[c, 0 : groups - 1], got.at[c, 0 : groups - 1], recv1.at[c]).wait()
        pltpu.make_async_copy(rows_for(gz, c, 0, planes), got.at[c, gz], own_sem.at[c]).wait()

    def span_chunk(c):
        def first(i, inner):
            rows = pl.ds(pl.multiple_of(i * 16, 16), 16)
            for lane in range(wide // 128):
                lanes = pl.ds(lane * 128, 128)
                s = [got[c, b, pl.ds(i * 2, 2), :, lanes].reshape(16, 128) for b in range(groups)]
                for p, pair in enumerate(sixteenths(s, s)):
                    for part in range(2):
                        at = pl.ds(part * wide + lane * 128, 128)
                        high[p, rows, at], low[p, rows, at] = split(pair[part])
            return inner

        lax.fori_loop(0, planes // 2, first, 0)

        def second(p, inner):
            value = dot(high[p], tables[0, p]) + dot(low[p], tables[0, p])
            result[p] = value + dot(high[p], tables[1, p])
            return inner

        lax.fori_loop(0, groups, second, 0)

        def third(t, inner):
            lanes = pl.ds(pl.multiple_of(t * 128, 128), 128)
            found = [result[p, :, lanes] for p in range(groups)]
            for odd in range(2):
                mixed = jnp.concatenate(
                    [
                        jnp.where(lower, found[2 * u + odd], found[2 * u + 1 - odd])
                        for u in range(groups // 2)
                    ],
                    axis=1,
                )
                top, rest = split(mixed)
                cosine[c, 2 * t + odd] = dot(top, orders[odd]) + dot(rest, orders[odd])
            return inner

        lax.fori_loop(0, groups // 2, third, 0)

    def mine(c, lanes):
        return pltpu.make_async_copy(
            cosine.at[c, gz, pl.ds(pl.multiple_of(gx * 8, 8), 8), lanes],
            pencil.at[gx * groups + gz, c, :, lanes],
            own2.at[c],
        )

    def send(c, slot, lanes):
        def one(t, inner):
            o = (t * STEP) % peers + 1
            to_x = (x_ring + (o // 8) % 4) % 4
            to_gz = ((z + o // 32) % 4) * 2 + to_x // 2
            to_gx = (to_x % 2) * 8 + ((y + (o // 2) % 4) % 4) * 2 + (core + o) % 2
            pltpu.make_async_remote_copy(
                src_ref=cosine.at[c, to_gz, pl.ds(pl.multiple_of(to_gx * 8, 8), 8), lanes],
                dst_ref=pencil.at[gx * groups + gz, c, :, lanes],
                send_sem=send2.at[slot],
                recv_sem=recv2.at[slot],
                device_id=(to_gz, to_gx),
                device_id_type=MESH,
            ).start()
            return inner

        lax.fori_loop(0, peers, one, 0)

    every = pl.ds(0, wide)
    block = wide // 2
    sides = [pl.ds(h * block, block) for h in range(2)]

    def early(c, carry):
        take(c)
        span_chunk(c)
        mine(c, every).start()
        send(c, c, every)
        return carry

    lax.fori_loop(0, last, early, 0)
    take(last)
    span_chunk(last)
    mine(last, every).start()
    for h in range(2):
        send(last, last + h, sides[h])

    periodic_copy = pltpu.make_async_copy(periodic_table, tables.at[0], table_sem.at[0])
    periodic_copy.start()
    pairs = planes // 2
    each = wide // 4
    main = 2 * last * groups * 8

    def fold(c, tiles):
        def step(i, carry):
            for lane in tiles:
                lanes = pl.ds(lane * 128, 128)
                s = [pencil[pl.ds(g * groups + i * 2, 2), c, :, lanes].reshape(16, 128) for g in range(planes)]
                even = [s[g] + s[g + pairs] for g in range(pairs)]
                odd = [s[g] - s[g + pairs] for g in range(pairs)]
                for p, pair in enumerate(sixteenths(even, odd)):
                    for part in range(2):
                        at = part * (groups * 8) + (main if c == last else part * (main // 2 - groups * 8) + c * (groups * 8)) + i * 16
                        top = pl.ds(pl.multiple_of(at, 16), 16)
                        rest = pl.ds(pl.multiple_of(at + wide, 16), 16)
                        tables[1, p, top, lanes], tables[1, p, rest, lanes] = split(pair[part])
            return carry

        lax.fori_loop(0, groups // 2, step, 0)

    def arrived(c, slot, lanes):
        view = pencil.at[0:peers, c, :, lanes]
        return pltpu.make_async_copy(view, view, recv2.at[slot])

    for c in range(last):
        arrived(c, c, every).wait()
        mine(c, every).wait()
        fold(c, range(wide // 128))
    periodic_copy.wait()

    def gather(p, carry):
        table_high, table_low = tables[0, p, 0:wide, 0:main], tables[0, p, wide : 2 * wide, 0:main]
        for side in sides:
            line_high, line_low = tables[1, p, 0:main, side], tables[1, p, wide : wide + main, side]
            value = dot(table_high, line_high) + dot(table_high, line_low) + dot(table_low, line_high)
            for k in range(4):
                piece = value[k * each : (k + 1) * each].reshape(planes, 8, block)
                got[p // 2, (p % 2) * 4 + k, :, :, side] = piece
        return carry

    lax.fori_loop(0, pairs, gather, 0)
    mine(last, every).wait()
    for h in range(2):
        arrived(last, last + h, sides[h]).wait()
        tiles = range(h * block // 128, (h + 1) * block // 128)
        fold(last, tiles)
        for p in range(pairs):
            table_high, table_low = tables[0, p, 0:wide, main:wide], tables[0, p, wide : 2 * wide, main:wide]
            line_high, line_low = tables[1, p, main:wide, sides[h]], tables[1, p, wide + main : 2 * wide, sides[h]]
            value = dot(
                jnp.concatenate([table_high, table_high], axis=1),
                jnp.concatenate([line_high, line_low], axis=0),
            ) + dot(table_low, line_high)
            for which in range(2):
                residue = (p, planes - p)[which] if p else (0, pairs)[which]
                for part in range(2):
                    k = 2 * which + part
                    before = got[p // 2, (p % 2) * 4 + k, :, :, sides[h]].reshape(each, block)
                    piece = value[k * each : (k + 1) * each] + before
                    for n, lane in enumerate(tiles):
                        at = pl.ds(residue, each, stride=planes)
                        stage[lane, part, at, :] = piece[:, n * 128 : n * 128 + 128]

    everything = got.at[:, 0 : groups - 1]
    pltpu.make_async_copy(everything, everything, send1).wait()
    for slot in range(CHUNKS + 1):
        lanes = every if slot < last else sides[slot - last]
        view = pencil.at[0:peers, min(slot, last), :, lanes]
        pltpu.make_async_copy(view, view, send2.at[slot]).wait()


def place(tiles, out, sems):
    copies = [
        pltpu.make_async_copy(
            tiles.at[lane, part], out.at[0, part, :, pl.ds(lane * 128, 128)], sems.at[lane, part]
        )
        for lane in range(tiles.shape[0])
        for part in range(2)
    ]
    for copy in copies:
        copy.start()
    for copy in copies:
        copy.wait()


def local(source):
    groups, across = lax.axis_size("gz"), lax.axis_size("gx")
    planes, rows, wide = source.shape
    span_total, periodic_total = wide * groups, rows * across
    factor = 1.0 / math.sqrt(span_total * periodic_total)
    table = jnp.asarray(span_tables(span_total, groups))
    order = jnp.asarray(order_tables(span_total, groups))
    periodic = jnp.asarray(periodic_tables(periodic_total, across, groups, factor))
    any_spec = pl.BlockSpec(memory_space=pl.ANY)
    lines = planes * 8
    half = periodic_total // 2
    tiles = pl.pallas_call(
        kernel,
        out_shape=pltpu.VMEM((wide // 128, 2, half, 128), F32),
        in_specs=[any_spec] * 4,
        out_specs=pl.BlockSpec(memory_space=pltpu.VMEM),
        scratch_shapes=[
            pltpu.VMEM((CHUNKS, groups, planes, 8, wide), F32),
            pltpu.VMEM(table.shape, BF16),
            pltpu.VMEM(order.shape, BF16),
            pltpu.VMEM((groups, lines, 2 * wide), BF16),
            pltpu.VMEM((groups, lines, 2 * wide), BF16),
            pltpu.VMEM((groups, lines, wide), F32),
            pltpu.VMEM((CHUNKS, groups, lines, wide), F32),
            pltpu.VMEM((across * groups, CHUNKS, 8, wide), F32),
            pltpu.SemaphoreType.DMA((2,)),
            pltpu.SemaphoreType.DMA((CHUNKS,)),
            pltpu.SemaphoreType.DMA,
            pltpu.SemaphoreType.DMA((CHUNKS,)),
            pltpu.SemaphoreType.DMA((CHUNKS + 1,)),
            pltpu.SemaphoreType.DMA((CHUNKS + 1,)),
            pltpu.SemaphoreType.DMA((CHUNKS,)),
        ],
        compiler_params=pltpu.CompilerParams(
            collective_id=0, has_side_effects=True, vmem_limit_bytes=48 * 2**20
        ),
        name="transform",
    )(source, table, order, periodic)
    return pl.pallas_call(
        place,
        out_shape=jax.ShapeDtypeStruct((1, 2, half, wide), F32),
        in_specs=[any_spec],
        out_specs=any_spec,
        scratch_shapes=[pltpu.SemaphoreType.DMA((wide // 128, 2))],
        compiler_params=pltpu.CompilerParams(vmem_limit_bytes=4 * 2**20),
        name="place",
    )(pltpu.with_memory_space_constraint(tiles, pltpu.VMEM))


def solution(mesh):
    return jax.shard_map(
        local,
        mesh=mesh,
        in_specs=(P(None, "gx", "gz"),),
        out_specs=P("gx", None, None, "gz"),
        check_vma=False,
    )
```

```python
import math

import jax
import jax.numpy as jnp
import ml_dtypes
import numpy as np
from jax import lax
from jax.experimental import pallas as pl
from jax.experimental.pallas import tpu as pltpu
from jax.sharding import PartitionSpec as P

MESH = pl.DeviceIdType.MESH
BF16 = jnp.bfloat16
F32 = jnp.float32
CHUNKS = 4
PIECES = 16
STEP = 33
BASE = 64


def halves(table):
    high = table.astype(np.float32).astype(ml_dtypes.bfloat16)
    low = (table - high.astype(np.float64)).astype(np.float32).astype(ml_dtypes.bfloat16)
    return np.stack([high, low])


def span_tables(length, groups):
    wide = length // groups
    turns = 2 * groups
    each = length // turns // groups
    offset = np.arange(wide)
    table = np.zeros((groups, 2, wide, groups // 2, 2, 2, each))
    for p in range(groups):
        for tile in range(groups // 2):
            for half in range(2):
                block = 2 * tile + (half ^ (p % 2))
                for which in range(2):
                    residue = (p, turns - p)[which] if p else (0, groups)[which]
                    k = residue + turns * (block * each + np.arange(each))
                    angle = math.pi / (2 * length) * (np.outer(2 * offset + 1, k) % (4 * length))
                    if p:
                        table[p, 0, :, tile, half, which] = 2 * np.cos(angle)
                        table[p, 1, :, tile, half, which] = 2 * np.sin(angle) * (1 - 2 * which)
                    else:
                        table[p, which, :, tile, half, which] = 2 * np.cos(angle)
    return halves(table.reshape(groups, 2 * wide, wide))


def order_tables(length, groups):
    wide = length // groups
    turns = 2 * groups
    each = wide // turns
    out = np.zeros((2, wide, wide), np.float32)
    for odd in range(2):
        row = 0
        for u in range(groups // 2):
            for half in range(2):
                p = 2 * u + (half ^ odd)
                for which in range(2):
                    residue = (p, turns - p)[which] if p else (0, groups)[which]
                    for j in range(each):
                        out[odd, row, j * turns + residue] = 1.0
                        row += 1
    return out.astype(ml_dtypes.bfloat16)


def periodic_tables(length, groups, spans, factor):
    wide = length // groups
    each = wide // 2
    rest = wide // spans // CHUNKS
    r = np.arange(wide).reshape(spans, CHUNKS, rest).transpose(1, 0, 2).reshape(-1)
    table = np.zeros((groups // 2, 2, 2, each, 2, wide))
    for p in range(groups // 2):
        for which in range(2):
            residue = (p, groups - p)[which] if p else (0, groups // 2)[which]
            q = residue + groups * np.arange(each)
            angle = 2 * math.pi / length * (np.outer(q, r) % length)
            cos, sin = np.cos(angle) * factor, np.sin(angle) * factor
            if p:
                sign = 1 - 2 * which
                table[p, which, 0, :, 0] = cos
                table[p, which, 0, :, 1] = sin * sign
                table[p, which, 1, :, 0] = -sin
                table[p, which, 1, :, 1] = cos * sign
            else:
                table[p, which, 0, :, which] = cos
                table[p, which, 1, :, which] = -sin
    table[0, 0, 1, 0, 0] = (1 - 2 * (r % 2)) * factor
    cut = wide - wide // CHUNKS
    table = table.reshape(groups // 2, 2 * wide, 2, wide)
    table = [t.reshape(groups // 2, 2 * wide, -1) for t in (table[..., :cut], table[..., cut:])]
    high, low = halves(np.concatenate(table, axis=-1))
    return np.concatenate([high, low], axis=1)


def split(value):
    high = value.astype(BF16)
    return high, (value - high.astype(F32)).astype(BF16)


def sixteenths(even, odd):
    root = math.sqrt(0.5)

    def parts(s):
        plus, minus = root * (s[1] + s[3]), root * (s[1] - s[3])
        return plus, minus

    out = [None] * 8
    s = even[0::2]
    t = even[1::2]
    p0, q0 = (s[0] + s[2]) + (s[1] + s[3]), (t[0] + t[2]) + (t[1] + t[3])
    p4, q4 = (s[0] + s[2]) - (s[1] + s[3]), (t[0] + t[2]) - (t[1] + t[3])
    out[0] = (p0 + q0, p0 - q0)
    out[4] = (p4, -q4)
    p2 = (s[0] - s[2], s[3] - s[1])
    q2 = (t[0] - t[2], t[3] - t[1])
    w2 = (root * (q2[0] + q2[1]), root * (q2[1] - q2[0]))
    out[2] = (p2[0] + w2[0], p2[1] + w2[1])
    out[6] = (p2[0] - w2[0], w2[1] - p2[1])
    s = odd[0::2]
    t = odd[1::2]
    s_plus, s_minus = parts(s)
    t_plus, t_minus = parts(t)
    p1, p3 = (s[0] + s_minus, -s[2] - s_plus), (s[0] - s_minus, s[2] - s_plus)
    q1, q3 = (t[0] + t_minus, -t[2] - t_plus), (t[0] - t_minus, t[2] - t_plus)
    for k, pk, qk in ((1, p1, q1), (3, p3, q3)):
        c, d = math.cos(math.pi * k / 8), math.sin(math.pi * k / 8)
        wk = (c * qk[0] + d * qk[1], c * qk[1] - d * qk[0])
        out[k] = (pk[0] + wk[0], pk[1] + wk[1])
        out[8 - k] = (pk[0] - wk[0], wk[1] - pk[1])
    return out


def dot(left, right):
    return jnp.dot(left, right, preferred_element_type=F32)


def kernel(
    source, span_table, order_table, periodic_table, stage, got, tables, orders, high, low, result, cosine, pencil,
    table_sem, own_sem, send1, recv1, send2, recv2, own2,
):
    gz, gx = lax.axis_index("gz"), lax.axis_index("gx")
    z, x_ring, y, core = gz // 2, (gz % 2) * 2 + gx // 8, (gx // 2) % 4, gx % 2
    groups, planes, wide = got.shape[1], got.shape[2], got.shape[4]
    peers = groups * planes - 1
    last = CHUNKS - 1

    def rows_for(group, c, start, size):
        return source.at[pl.ds(start, size), pl.ds(pl.multiple_of(group * (CHUNKS * 8) + c * 8, 8), 8), :]

    barrier = pltpu.get_barrier_semaphore()

    def greet_span(t, carry):
        pl.semaphore_signal(barrier, inc=1, device_id=((gz + t) % groups, gx), device_id_type=MESH)
        return carry

    def greet_planes(t, carry):
        pl.semaphore_signal(barrier, inc=1, device_id=(gz, (gx + t) % planes), device_id_type=MESH)
        return carry

    lax.fori_loop(1, groups, greet_span, 0)
    lax.fori_loop(1, planes, greet_planes, 0)
    for c in range(CHUNKS):
        pltpu.make_async_copy(rows_for(gz, c, 0, planes), got.at[c, gz], own_sem.at[c]).start()
    table_copy = pltpu.make_async_copy(span_table, tables, table_sem.at[0])
    order_copy = pltpu.make_async_copy(order_table, orders, table_sem.at[1])
    table_copy.start()
    order_copy.start()
    pl.semaphore_wait(barrier, groups + planes - 2)

    size = planes // PIECES

    def scatter(i, carry):
        c, start, t = i // (groups - 1) // PIECES, (i // (groups - 1)) % PIECES * size, i % (groups - 1) + 1
        to = ((z + t // 2) % 4) * 2 + (gz + t) % 2
        pltpu.make_async_remote_copy(
            src_ref=rows_for(to, c, start, size),
            dst_ref=got.at[c, gz, pl.ds(start, size)],
            send_sem=send1,
            recv_sem=recv1.at[c],
            device_id=(to, gx),
            device_id_type=MESH,
        ).start()
        return carry

    each_chunk = PIECES * (groups - 1)
    lax.fori_loop(0, 2 * each_chunk, scatter, 0)
    table_copy.wait()
    order_copy.wait()

    lower = lax.broadcasted_iota(jnp.int32, (planes * 8, 128), 1) < 64

    def take(c):
        pltpu.make_async_copy(got.at[c, 0 : groups - 1], got.at[c, 0 : groups - 1], recv1.at[c]).wait()
        pltpu.make_async_copy(rows_for(gz, c, 0, planes), got.at[c, gz], own_sem.at[c]).wait()

    def span_chunk(c):
        def first(i, inner):
            rows = pl.ds(pl.multiple_of(i * 16, 16), 16)
            for lane in range(wide // 128):
                lanes = pl.ds(lane * 128, 128)
                s = [got[c, b, pl.ds(i * 2, 2), :, lanes].reshape(16, 128) for b in range(groups)]
                for p, pair in enumerate(sixteenths(s, s)):
                    for part in range(2):
                        at = pl.ds(part * wide + lane * 128, 128)
                        high[p, rows, at], low[p, rows, at] = split(pair[part])
            return inner

        lax.fori_loop(0, planes // 2, first, 0)

        def second(p, inner):
            value = dot(high[p], tables[0, p]) + dot(low[p], tables[0, p])
            result[p] = value + dot(high[p], tables[1, p])
            return inner

        lax.fori_loop(0, groups, second, 0)

        def third(t, inner):
            lanes = pl.ds(pl.multiple_of(t * 128, 128), 128)
            found = [result[p, :, lanes] for p in range(groups)]
            for odd in range(2):
                mixed = jnp.concatenate(
                    [
                        jnp.where(lower, found[2 * u + odd], found[2 * u + 1 - odd])
                        for u in range(groups // 2)
                    ],
                    axis=1,
                )
                top, rest = split(mixed)
                cosine[c, 2 * t + odd] = dot(top, orders[odd]) + dot(rest, orders[odd])
            return inner

        lax.fori_loop(0, groups // 2, third, 0)

    def mine(c, lanes):
        return pltpu.make_async_copy(
            cosine.at[c, gz, pl.ds(pl.multiple_of(gx * 8, 8), 8), lanes],
            pencil.at[gx * groups + gz, c, :, lanes],
            own2.at[c],
        )

    def send(c, slot, lanes):
        def one(t, inner):
            o = (t * STEP + BASE) % peers + 1
            to_x = (x_ring + (o // 8) % 4) % 4
            to_gz = ((z + o // 32) % 4) * 2 + to_x // 2
            to_gx = (to_x % 2) * 8 + ((y + (o // 2) % 4) % 4) * 2 + (core + o) % 2
            pltpu.make_async_remote_copy(
                src_ref=cosine.at[c, to_gz, pl.ds(pl.multiple_of(to_gx * 8, 8), 8), lanes],
                dst_ref=pencil.at[gx * groups + gz, c, :, lanes],
                send_sem=send2.at[slot],
                recv_sem=recv2.at[slot],
                device_id=(to_gz, to_gx),
                device_id_type=MESH,
            ).start()
            return inner

        lax.fori_loop(0, peers, one, 0)

    every = pl.ds(0, wide)
    block = wide // 2
    sides = [pl.ds(h * block, block) for h in range(2)]

    def early(c, carry):
        take(c)

        @pl.when(c + 2 < CHUNKS)
        def _():
            lax.fori_loop((c + 2) * each_chunk, (c + 3) * each_chunk, scatter, 0)

        span_chunk(c)
        mine(c, every).start()
        send(c, c, every)
        return carry

    lax.fori_loop(0, last, early, 0)
    take(last)
    span_chunk(last)
    mine(last, every).start()
    for h in range(2):
        send(last, last + h, sides[h])

    periodic_copy = pltpu.make_async_copy(periodic_table, tables.at[0], table_sem.at[0])
    periodic_copy.start()
    pairs = planes // 2
    each = wide // 4
    main = 2 * last * groups * 8

    def fold(c, tiles):
        def step(i, carry):
            for lane in tiles:
                lanes = pl.ds(lane * 128, 128)
                s = [pencil[pl.ds(g * groups + i * 2, 2), c, :, lanes].reshape(16, 128) for g in range(planes)]
                even = [s[g] + s[g + pairs] for g in range(pairs)]
                odd = [s[g] - s[g + pairs] for g in range(pairs)]
                for p, pair in enumerate(sixteenths(even, odd)):
                    for part in range(2):
                        at = part * (groups * 8) + (main if c == last else part * (main // 2 - groups * 8) + c * (groups * 8)) + i * 16
                        top = pl.ds(pl.multiple_of(at, 16), 16)
                        rest = pl.ds(pl.multiple_of(at + wide, 16), 16)
                        tables[1, p, top, lanes], tables[1, p, rest, lanes] = split(pair[part])
            return carry

        lax.fori_loop(0, groups // 2, step, 0)

    def arrived(c, slot, lanes):
        view = pencil.at[0:peers, c, :, lanes]
        return pltpu.make_async_copy(view, view, recv2.at[slot])

    for c in range(last):
        arrived(c, c, every).wait()
        mine(c, every).wait()
        fold(c, range(wide // 128))
    periodic_copy.wait()

    def gather(p, carry):
        table_high, table_low = tables[0, p, 0:wide, 0:main], tables[0, p, wide : 2 * wide, 0:main]
        for side in sides:
            line_high, line_low = tables[1, p, 0:main, side], tables[1, p, wide : wide + main, side]
            value = dot(table_high, line_high) + dot(table_high, line_low) + dot(table_low, line_high)
            for k in range(4):
                piece = value[k * each : (k + 1) * each].reshape(planes, 8, block)
                got[p // 2, (p % 2) * 4 + k, :, :, side] = piece
        return carry

    lax.fori_loop(0, pairs, gather, 0)
    mine(last, every).wait()
    for h in range(2):
        arrived(last, last + h, sides[h]).wait()
        tiles = range(h * block // 128, (h + 1) * block // 128)
        fold(last, tiles)
        for p in range(pairs):
            table_high, table_low = tables[0, p, 0:wide, main:wide], tables[0, p, wide : 2 * wide, main:wide]
            line_high, line_low = tables[1, p, main:wide, sides[h]], tables[1, p, wide + main : 2 * wide, sides[h]]
            value = dot(
                jnp.concatenate([table_high, table_high, table_low], axis=1),
                jnp.concatenate([line_high, line_low, line_high], axis=0),
            )
            for which in range(2):
                residue = (p, planes - p)[which] if p else (0, pairs)[which]
                for part in range(2):
                    k = 2 * which + part
                    before = got[p // 2, (p % 2) * 4 + k, :, :, sides[h]].reshape(each, block)
                    piece = value[k * each : (k + 1) * each] + before
                    for n, lane in enumerate(tiles):
                        at = pl.ds(residue, each, stride=planes)
                        stage[lane, part, at, :] = piece[:, n * 128 : n * 128 + 128]

    everything = got.at[:, 0 : groups - 1]
    pltpu.make_async_copy(everything, everything, send1).wait()
    for slot in range(CHUNKS + 1):
        lanes = every if slot < last else sides[slot - last]
        view = pencil.at[0:peers, min(slot, last), :, lanes]
        pltpu.make_async_copy(view, view, send2.at[slot]).wait()


def place(tiles, out, sems):
    copies = [
        pltpu.make_async_copy(
            tiles.at[lane, part], out.at[0, part, :, pl.ds(lane * 128, 128)], sems.at[lane, part]
        )
        for lane in range(tiles.shape[0])
        for part in range(2)
    ]
    for copy in copies:
        copy.start()
    for copy in copies:
        copy.wait()


def local(source):
    groups, across = lax.axis_size("gz"), lax.axis_size("gx")
    planes, rows, wide = source.shape
    span_total, periodic_total = wide * groups, rows * across
    factor = 1.0 / math.sqrt(span_total * periodic_total)
    table = jnp.asarray(span_tables(span_total, groups))
    order = jnp.asarray(order_tables(span_total, groups))
    periodic = jnp.asarray(periodic_tables(periodic_total, across, groups, factor))
    any_spec = pl.BlockSpec(memory_space=pl.ANY)
    lines = planes * 8
    half = periodic_total // 2
    tiles = pl.pallas_call(
        kernel,
        out_shape=pltpu.VMEM((wide // 128, 2, half, 128), F32),
        in_specs=[any_spec] * 4,
        out_specs=pl.BlockSpec(memory_space=pltpu.VMEM),
        scratch_shapes=[
            pltpu.VMEM((CHUNKS, groups, planes, 8, wide), F32),
            pltpu.VMEM(table.shape, BF16),
            pltpu.VMEM(order.shape, BF16),
            pltpu.VMEM((groups, lines, 2 * wide), BF16),
            pltpu.VMEM((groups, lines, 2 * wide), BF16),
            pltpu.VMEM((groups, lines, wide), F32),
            pltpu.VMEM((CHUNKS, groups, lines, wide), F32),
            pltpu.VMEM((across * groups, CHUNKS, 8, wide), F32),
            pltpu.SemaphoreType.DMA((2,)),
            pltpu.SemaphoreType.DMA((CHUNKS,)),
            pltpu.SemaphoreType.DMA,
            pltpu.SemaphoreType.DMA((CHUNKS,)),
            pltpu.SemaphoreType.DMA((CHUNKS + 1,)),
            pltpu.SemaphoreType.DMA((CHUNKS + 1,)),
            pltpu.SemaphoreType.DMA((CHUNKS,)),
        ],
        compiler_params=pltpu.CompilerParams(
            collective_id=0, has_side_effects=True, vmem_limit_bytes=48 * 2**20
        ),
        name="transform",
    )(source, table, order, periodic)
    return pl.pallas_call(
        place,
        out_shape=jax.ShapeDtypeStruct((1, 2, half, wide), F32),
        in_specs=[any_spec],
        out_specs=any_spec,
        scratch_shapes=[pltpu.SemaphoreType.DMA((wide // 128, 2))],
        compiler_params=pltpu.CompilerParams(vmem_limit_bytes=4 * 2**20),
        name="place",
    )(pltpu.with_memory_space_constraint(tiles, pltpu.VMEM))


def solution(mesh):
    return jax.shard_map(
        local,
        mesh=mesh,
        in_specs=(P(None, "gx", "gz"),),
        out_specs=P("gx", None, None, "gz"),
        check_vma=False,
    )
```

```python
import math

import jax
import jax.numpy as jnp
import ml_dtypes
import numpy as np
from jax import lax
from jax.experimental import pallas as pl
from jax.experimental.pallas import tpu as pltpu
from jax.sharding import PartitionSpec as P

MESH = pl.DeviceIdType.MESH
BF16 = jnp.bfloat16
F32 = jnp.float32
CHUNKS = 4
PIECES = 8
STEP = 33
BASE = 64


def halves(table):
    high = table.astype(np.float32).astype(ml_dtypes.bfloat16)
    low = (table - high.astype(np.float64)).astype(np.float32).astype(ml_dtypes.bfloat16)
    return np.stack([high, low])


def span_tables(length, groups):
    wide = length // groups
    turns = 2 * groups
    each = length // turns // groups
    offset = np.arange(wide)
    table = np.zeros((groups, 2, wide, groups // 2, 2, 2, each))
    for p in range(groups):
        for tile in range(groups // 2):
            for half in range(2):
                block = 2 * tile + (half ^ (p % 2))
                for which in range(2):
                    residue = (p, turns - p)[which] if p else (0, groups)[which]
                    k = residue + turns * (block * each + np.arange(each))
                    angle = math.pi / (2 * length) * (np.outer(2 * offset + 1, k) % (4 * length))
                    if p:
                        table[p, 0, :, tile, half, which] = 2 * np.cos(angle)
                        table[p, 1, :, tile, half, which] = 2 * np.sin(angle) * (1 - 2 * which)
                    else:
                        table[p, which, :, tile, half, which] = 2 * np.cos(angle)
    return halves(table.reshape(groups, 2 * wide, wide))


def order_tables(length, groups):
    wide = length // groups
    turns = 2 * groups
    each = wide // turns
    out = np.zeros((2, wide, wide), np.float32)
    for odd in range(2):
        row = 0
        for u in range(groups // 2):
            for half in range(2):
                p = 2 * u + (half ^ odd)
                for which in range(2):
                    residue = (p, turns - p)[which] if p else (0, groups)[which]
                    for j in range(each):
                        out[odd, row, j * turns + residue] = 1.0
                        row += 1
    return out.astype(ml_dtypes.bfloat16)


def periodic_tables(length, groups, spans, factor):
    wide = length // groups
    each = wide // 2
    rest = wide // spans // CHUNKS
    r = np.arange(wide).reshape(spans, CHUNKS, rest).transpose(1, 0, 2).reshape(-1)
    table = np.zeros((groups // 2, 2, 2, each, 2, wide))
    for p in range(groups // 2):
        for which in range(2):
            residue = (p, groups - p)[which] if p else (0, groups // 2)[which]
            q = residue + groups * np.arange(each)
            angle = 2 * math.pi / length * (np.outer(q, r) % length)
            cos, sin = np.cos(angle) * factor, np.sin(angle) * factor
            if p:
                sign = 1 - 2 * which
                table[p, which, 0, :, 0] = cos
                table[p, which, 0, :, 1] = sin * sign
                table[p, which, 1, :, 0] = -sin
                table[p, which, 1, :, 1] = cos * sign
            else:
                table[p, which, 0, :, which] = cos
                table[p, which, 1, :, which] = -sin
    table[0, 0, 1, 0, 0] = (1 - 2 * (r % 2)) * factor
    cut = wide - wide // CHUNKS
    table = table.reshape(groups // 2, 2 * wide, 2, wide)
    table = [t.reshape(groups // 2, 2 * wide, -1) for t in (table[..., :cut], table[..., cut:])]
    high, low = halves(np.concatenate(table, axis=-1))
    return np.concatenate([high, low], axis=1)


def split(value):
    high = value.astype(BF16)
    return high, (value - high.astype(F32)).astype(BF16)


def sixteenths(even, odd):
    root = math.sqrt(0.5)

    def parts(s):
        plus, minus = root * (s[1] + s[3]), root * (s[1] - s[3])
        return plus, minus

    out = [None] * 8
    s = even[0::2]
    t = even[1::2]
    p0, q0 = (s[0] + s[2]) + (s[1] + s[3]), (t[0] + t[2]) + (t[1] + t[3])
    p4, q4 = (s[0] + s[2]) - (s[1] + s[3]), (t[0] + t[2]) - (t[1] + t[3])
    out[0] = (p0 + q0, p0 - q0)
    out[4] = (p4, -q4)
    p2 = (s[0] - s[2], s[3] - s[1])
    q2 = (t[0] - t[2], t[3] - t[1])
    w2 = (root * (q2[0] + q2[1]), root * (q2[1] - q2[0]))
    out[2] = (p2[0] + w2[0], p2[1] + w2[1])
    out[6] = (p2[0] - w2[0], w2[1] - p2[1])
    s = odd[0::2]
    t = odd[1::2]
    s_plus, s_minus = parts(s)
    t_plus, t_minus = parts(t)
    p1, p3 = (s[0] + s_minus, -s[2] - s_plus), (s[0] - s_minus, s[2] - s_plus)
    q1, q3 = (t[0] + t_minus, -t[2] - t_plus), (t[0] - t_minus, t[2] - t_plus)
    for k, pk, qk in ((1, p1, q1), (3, p3, q3)):
        c, d = math.cos(math.pi * k / 8), math.sin(math.pi * k / 8)
        wk = (c * qk[0] + d * qk[1], c * qk[1] - d * qk[0])
        out[k] = (pk[0] + wk[0], pk[1] + wk[1])
        out[8 - k] = (pk[0] - wk[0], wk[1] - pk[1])
    return out


def dot(left, right):
    return jnp.dot(left, right, preferred_element_type=F32)


def kernel(
    source, span_table, order_table, periodic_table, stage, got, tables, orders, high, low, result, cosine, pencil,
    table_sem, own_sem, send1, recv1, send2, recv2, own2,
):
    gz, gx = lax.axis_index("gz"), lax.axis_index("gx")
    z, x_ring, y, core = gz // 2, (gz % 2) * 2 + gx // 8, (gx // 2) % 4, gx % 2
    groups, planes, wide = got.shape[1], got.shape[2], got.shape[4]
    peers = groups * planes - 1
    last = CHUNKS - 1

    def rows_for(group, c, start, size):
        return source.at[pl.ds(start, size), pl.ds(pl.multiple_of(group * (CHUNKS * 8) + c * 8, 8), 8), :]

    barrier = pltpu.get_barrier_semaphore()

    def greet_span(t, carry):
        pl.semaphore_signal(barrier, inc=1, device_id=((gz + t) % groups, gx), device_id_type=MESH)
        return carry

    def greet_planes(t, carry):
        pl.semaphore_signal(barrier, inc=1, device_id=(gz, (gx + t) % planes), device_id_type=MESH)
        return carry

    lax.fori_loop(1, groups, greet_span, 0)
    lax.fori_loop(1, planes, greet_planes, 0)
    for c in range(CHUNKS):
        pltpu.make_async_copy(rows_for(gz, c, 0, planes), got.at[c, gz], own_sem.at[c]).start()
    table_copy = pltpu.make_async_copy(span_table, tables, table_sem.at[0])
    order_copy = pltpu.make_async_copy(order_table, orders, table_sem.at[1])
    table_copy.start()
    order_copy.start()
    pl.semaphore_wait(barrier, groups + planes - 2)

    size = planes // PIECES

    def scatter(i, carry):
        c, start, t = i // (groups - 1) // PIECES, (i // (groups - 1)) % PIECES * size, i % (groups - 1) + 1
        to = ((z + t // 2) % 4) * 2 + (gz + t) % 2
        pltpu.make_async_remote_copy(
            src_ref=rows_for(to, c, start, size),
            dst_ref=got.at[c, gz, pl.ds(start, size)],
            send_sem=send1,
            recv_sem=recv1.at[c],
            device_id=(to, gx),
            device_id_type=MESH,
        ).start()
        return carry

    each_chunk = PIECES * (groups - 1)
    lax.fori_loop(0, 2 * each_chunk, scatter, 0)
    table_copy.wait()
    order_copy.wait()

    lower = lax.broadcasted_iota(jnp.int32, (planes * 8, 128), 1) < 64

    def take(c):
        pltpu.make_async_copy(got.at[c, 0 : groups - 1], got.at[c, 0 : groups - 1], recv1.at[c]).wait()
        pltpu.make_async_copy(rows_for(gz, c, 0, planes), got.at[c, gz], own_sem.at[c]).wait()

    def span_chunk(c):
        def first(i, inner):
            rows = pl.ds(pl.multiple_of(i * 16, 16), 16)
            for lane in range(wide // 128):
                lanes = pl.ds(lane * 128, 128)
                s = [got[c, b, pl.ds(i * 2, 2), :, lanes].reshape(16, 128) for b in range(groups)]
                for p, pair in enumerate(sixteenths(s, s)):
                    for part in range(2):
                        at = pl.ds(part * wide + lane * 128, 128)
                        high[p, rows, at], low[p, rows, at] = split(pair[part])
            return inner

        lax.fori_loop(0, planes // 2, first, 0)

        def second(p, inner):
            value = dot(high[p], tables[0, p]) + dot(low[p], tables[0, p])
            result[p] = value + dot(high[p], tables[1, p])
            return inner

        lax.fori_loop(0, groups, second, 0)

        def third(t, inner):
            lanes = pl.ds(pl.multiple_of(t * 128, 128), 128)
            found = [result[p, :, lanes] for p in range(groups)]
            for odd in range(2):
                mixed = jnp.concatenate(
                    [
                        jnp.where(lower, found[2 * u + odd], found[2 * u + 1 - odd])
                        for u in range(groups // 2)
                    ],
                    axis=1,
                )
                top, rest = split(mixed)
                cosine[c, 2 * t + odd] = dot(top, orders[odd]) + dot(rest, orders[odd])
            return inner

        lax.fori_loop(0, groups // 2, third, 0)

    def mine(c, lanes):
        return pltpu.make_async_copy(
            cosine.at[c, gz, pl.ds(pl.multiple_of(gx * 8, 8), 8), lanes],
            pencil.at[gx * groups + gz, c, :, lanes],
            own2.at[c],
        )

    def send(c, slot, lanes):
        def one(t, inner):
            o = (t * STEP + BASE) % peers + 1
            to_x = (x_ring + (o // 8) % 4) % 4
            to_gz = ((z + o // 32) % 4) * 2 + to_x // 2
            to_gx = (to_x % 2) * 8 + ((y + (o // 2) % 4) % 4) * 2 + (core + o) % 2
            pltpu.make_async_remote_copy(
                src_ref=cosine.at[c, to_gz, pl.ds(pl.multiple_of(to_gx * 8, 8), 8), lanes],
                dst_ref=pencil.at[gx * groups + gz, c, :, lanes],
                send_sem=send2.at[slot],
                recv_sem=recv2.at[slot],
                device_id=(to_gz, to_gx),
                device_id_type=MESH,
            ).start()
            return inner

        lax.fori_loop(0, peers, one, 0)

    every = pl.ds(0, wide)
    block = wide // 2
    sides = [pl.ds(h * block, block) for h in range(2)]

    def early(c, carry):
        take(c)

        @pl.when(c + 2 < CHUNKS)
        def _():
            lax.fori_loop((c + 2) * each_chunk, (c + 3) * each_chunk, scatter, 0)

        span_chunk(c)
        mine(c, every).start()
        send(c, c, every)
        return carry

    lax.fori_loop(0, last, early, 0)
    take(last)
    span_chunk(last)
    mine(last, every).start()
    for h in range(2):
        send(last, last + h, sides[h])

    periodic_copy = pltpu.make_async_copy(periodic_table, tables.at[0], table_sem.at[0])
    periodic_copy.start()
    pairs = planes // 2
    each = wide // 4
    main = 2 * last * groups * 8

    def fold(c, tiles):
        def step(i, carry):
            for lane in tiles:
                lanes = pl.ds(lane * 128, 128)
                s = [pencil[pl.ds(g * groups + i * 2, 2), c, :, lanes].reshape(16, 128) for g in range(planes)]
                even = [s[g] + s[g + pairs] for g in range(pairs)]
                odd = [s[g] - s[g + pairs] for g in range(pairs)]
                for p, pair in enumerate(sixteenths(even, odd)):
                    for part in range(2):
                        at = part * (groups * 8) + (main if c == last else part * (main // 2 - groups * 8) + c * (groups * 8)) + i * 16
                        top = pl.ds(pl.multiple_of(at, 16), 16)
                        rest = pl.ds(pl.multiple_of(at + wide, 16), 16)
                        tables[1, p, top, lanes], tables[1, p, rest, lanes] = split(pair[part])
            return carry

        lax.fori_loop(0, groups // 2, step, 0)

    def arrived(c, slot, lanes):
        view = pencil.at[0:peers, c, :, lanes]
        return pltpu.make_async_copy(view, view, recv2.at[slot])

    for c in range(last):
        arrived(c, c, every).wait()
        mine(c, every).wait()
        fold(c, range(wide // 128))
    periodic_copy.wait()

    def gather(p, carry):
        table_high, table_low = tables[0, p, 0:wide, 0:main], tables[0, p, wide : 2 * wide, 0:main]
        for side in sides:
            line_high, line_low = tables[1, p, 0:main, side], tables[1, p, wide : wide + main, side]
            value = dot(table_high, line_high) + dot(table_high, line_low) + dot(table_low, line_high)
            for k in range(4):
                piece = value[k * each : (k + 1) * each].reshape(planes, 8, block)
                got[p // 2, (p % 2) * 4 + k, :, :, side] = piece
        return carry

    lax.fori_loop(0, pairs, gather, 0)
    mine(last, every).wait()
    for h in range(2):
        arrived(last, last + h, sides[h]).wait()
        tiles = range(h * block // 128, (h + 1) * block // 128)
        fold(last, tiles)
        for p in range(pairs):
            table_high, table_low = tables[0, p, 0:wide, main:wide], tables[0, p, wide : 2 * wide, main:wide]
            line_high, line_low = tables[1, p, main:wide, sides[h]], tables[1, p, wide + main : 2 * wide, sides[h]]
            value = dot(
                jnp.concatenate([table_high, table_high, table_low], axis=1),
                jnp.concatenate([line_high, line_low, line_high], axis=0),
            )
            for which in range(2):
                residue = (p, planes - p)[which] if p else (0, pairs)[which]
                for part in range(2):
                    k = 2 * which + part
                    before = got[p // 2, (p % 2) * 4 + k, :, :, sides[h]].reshape(each, block)
                    piece = value[k * each : (k + 1) * each] + before
                    for n, lane in enumerate(tiles):
                        at = pl.ds(residue, each, stride=planes)
                        stage[lane, part, at, :] = piece[:, n * 128 : n * 128 + 128]

    everything = got.at[:, 0 : groups - 1]
    pltpu.make_async_copy(everything, everything, send1).wait()
    for slot in range(CHUNKS + 1):
        lanes = every if slot < last else sides[slot - last]
        view = pencil.at[0:peers, min(slot, last), :, lanes]
        pltpu.make_async_copy(view, view, send2.at[slot]).wait()


def place(tiles, out, sems):
    copies = [
        pltpu.make_async_copy(
            tiles.at[lane, part], out.at[0, part, :, pl.ds(lane * 128, 128)], sems.at[lane, part]
        )
        for lane in range(tiles.shape[0])
        for part in range(2)
    ]
    for copy in copies:
        copy.start()
    for copy in copies:
        copy.wait()


def local(source):
    groups, across = lax.axis_size("gz"), lax.axis_size("gx")
    planes, rows, wide = source.shape
    span_total, periodic_total = wide * groups, rows * across
    factor = 1.0 / math.sqrt(span_total * periodic_total)
    table = jnp.asarray(span_tables(span_total, groups))
    order = jnp.asarray(order_tables(span_total, groups))
    periodic = jnp.asarray(periodic_tables(periodic_total, across, groups, factor))
    any_spec = pl.BlockSpec(memory_space=pl.ANY)
    lines = planes * 8
    half = periodic_total // 2
    tiles = pl.pallas_call(
        kernel,
        out_shape=pltpu.VMEM((wide // 128, 2, half, 128), F32),
        in_specs=[any_spec] * 4,
        out_specs=pl.BlockSpec(memory_space=pltpu.VMEM),
        scratch_shapes=[
            pltpu.VMEM((CHUNKS, groups, planes, 8, wide), F32),
            pltpu.VMEM(table.shape, BF16),
            pltpu.VMEM(order.shape, BF16),
            pltpu.VMEM((groups, lines, 2 * wide), BF16),
            pltpu.VMEM((groups, lines, 2 * wide), BF16),
            pltpu.VMEM((groups, lines, wide), F32),
            pltpu.VMEM((CHUNKS, groups, lines, wide), F32),
            pltpu.VMEM((across * groups, CHUNKS, 8, wide), F32),
            pltpu.SemaphoreType.DMA((2,)),
            pltpu.SemaphoreType.DMA((CHUNKS,)),
            pltpu.SemaphoreType.DMA,
            pltpu.SemaphoreType.DMA((CHUNKS,)),
            pltpu.SemaphoreType.DMA((CHUNKS + 1,)),
            pltpu.SemaphoreType.DMA((CHUNKS + 1,)),
            pltpu.SemaphoreType.DMA((CHUNKS,)),
        ],
        compiler_params=pltpu.CompilerParams(
            collective_id=0, has_side_effects=True, vmem_limit_bytes=48 * 2**20
        ),
        name="transform",
    )(source, table, order, periodic)
    return pl.pallas_call(
        place,
        out_shape=jax.ShapeDtypeStruct((1, 2, half, wide), F32),
        in_specs=[any_spec],
        out_specs=any_spec,
        scratch_shapes=[pltpu.SemaphoreType.DMA((wide // 128, 2))],
        compiler_params=pltpu.CompilerParams(vmem_limit_bytes=4 * 2**20),
        name="place",
    )(pltpu.with_memory_space_constraint(tiles, pltpu.VMEM))


def solution(mesh):
    return jax.shard_map(
        local,
        mesh=mesh,
        in_specs=(P(None, "gx", "gz"),),
        out_specs=P("gx", None, None, "gz"),
        check_vma=False,
    )
```
